32 devices in a mesh: space: 8 (over z, core), chaos: 4 (over y, x).
Axes of the slice: x: 2, y: 2, z: 4, core: 2. Of those that a mesh axis runs over, the one named last changes fastest.
Arguments:
- chaos_modes: float32 [84, 32768], P(None, ('space', 'chaos')), may hold values from -0.2 to 0.2
- newton_heading: float32 [84, 32768], P(None, ('space', 'chaos')), may hold values from -0.2 to 0.2
- source: float32 [32768], P(('space', 'chaos')), may hold values from -6 to 6
- nodes: float32 [512, 6], replicated, may hold values from -3 to 3
- weights: float32 [512], replicated, may hold values from 0.0009765625 to 0.0029296875
- k_ref: float32 [4], replicated, may hold values from 0.5 to 4
- sensitivity: float32 [4, 6], replicated, may hold values from -0.1 to 0.1
- decay: float32 [4], replicated, may hold values from 0.1 to 0.5
- material: int32 [512], P('space'), may hold values from 0 to 3
- neighbors: int32 [512, 4], P('space'), may hold values from -1 to 79, as said below
- send_list: int32 [8, 8, 2], P('space'), may hold values from 0 to 63, as said below
Outputs:
- residual: float32 [84, 32768], P(None, ('space', 'chaos'))
- jvp_out: float32 [84, 32768], P(None, ('space', 'chaos'))
The draws below stay inside these ranges and needn't reach their ends.
Inputs may be any that keep to these rules, and one draw needn't show every extreme that they name: `neighbors`: -1 marks a face without neighbour. An entry below 64 is a block of the same partition; an entry 64 + t * 2 + j names slot j of what partition t sends here, where t is one or two indices away along space, cyclically, and the slot is live. send_list[s, t, j] is a local block of partition s. Only slots named by some neighbour entry are live: from s to a partition one or two indices away, cyclically, between 1 and 2 leading slots; to any other partition none.
All inputs are finite; a program needn't handle non-finite values.
Results may differ from the reference program's by a relative error of at most 0.0003.
Values sent between devices are 32-bit elements; how exact they have to be, the bound alone decides.
A program may use at most 192 MiB of HBM per device.

```python
import math
import jax
import jax.numpy as jnp
import numpy as np
from jax import lax

DIMS = 6
P_SIZE = 84
NMAT = 4
SEGMENT_SITES = 64
GAUSS_POINTS = 128
HMAX = 2
NB = 64
Q = 512
CELLS = 32768
N_SPACE = 8
N_CHAOS = 4


def halo_counts(key):
    count_key = jax.random.fold_in(key, 7)
    first_key, second_key = jax.random.split(count_key)
    sender = jnp.arange(N_SPACE, dtype=jnp.int32)[:, None]
    receiver = jnp.arange(N_SPACE, dtype=jnp.int32)[None, :]
    forward = (receiver - sender) % N_SPACE
    backward = (sender - receiver) % N_SPACE
    nearby = (forward == 1) | (forward == 2) | (backward == 1) | (backward == 2)
    counts = jax.random.randint(first_key, (N_SPACE, N_SPACE), 1, HMAX + 1, dtype=jnp.int32)
    chosen = jax.random.randint(second_key, (), 0, N_SPACE, dtype=jnp.int32)
    counts = jnp.where((sender == chosen) & (receiver == (chosen + 1) % N_SPACE), HMAX, counts)
    counts = jnp.where((sender == N_SPACE - 1) & (receiver == 0), HMAX, counts)
    return jnp.where(nearby, counts, 0)


def draw_send_list(key, part):
    return jax.random.randint(jax.random.fold_in(key, 11), (N_SPACE, N_SPACE, HMAX), 0, NB, dtype=jnp.int32)


def draw_neighbors(key, part):
    counts = halo_counts(key)
    local_key = jax.random.fold_in(key, 13)
    boundary_key = jax.random.fold_in(key, 17)
    block_ids = jnp.arange(NB, dtype=jnp.int32)[None, :, None]
    offsets = jax.random.randint(local_key, (N_SPACE, NB, 4), 1, NB, dtype=jnp.int32)
    local_ref = (block_ids + offsets) % NB
    boundary = jax.random.randint(boundary_key, (N_SPACE, NB, 4), 0, 8, dtype=jnp.int32) == 0
    local_ref = jnp.where(boundary, -1, local_ref)
    owner_rank = jnp.arange(N_SPACE, dtype=jnp.int32)[:, None]
    blocks = jnp.arange(NB, dtype=jnp.int32)[None, :]
    group_index = jnp.minimum(blocks // HMAX, 3)
    slot_index = blocks % HMAX
    stride = jnp.where(group_index == 0, -1, jnp.where(group_index == 1, 1, jnp.where(group_index == 2, -2, 2)))
    peer_rank = (owner_rank + stride) % N_SPACE
    live = (blocks < 4 * HMAX) & (slot_index < counts[peer_rank, owner_rank])
    halo_ref = NB + peer_rank * HMAX + slot_index
    face_three = jnp.where(live, halo_ref, local_ref[:, :, 3])
    result = local_ref.at[:, :, 3].set(face_three)
    return result.reshape(N_SPACE * NB, 4)


def place_ends(entries, own_key, least, largest):
    spot = [jax.random.randint(jax.random.fold_in(own_key, axis), (), 0, length) for axis, length in enumerate(entries.shape)]
    longest = entries.shape.index(max(entries.shape))
    next_to = spot[:longest] + [(spot[longest] + 1) % entries.shape[longest]] + spot[longest + 1:]
    return entries.at[tuple(spot)].set(least).at[tuple(next_to)].set(largest)


def block_levels(own_key, shape, pieces, least, top_value):
    def one(position, parts):
        draws = jax.random.uniform(jax.random.fold_in(jax.random.fold_in(own_key, 6), position), (parts,), jnp.float32, least / len(pieces), top_value / len(pieces))
        return jnp.repeat(jnp.exp(draws), shape[position] // parts).reshape((-1,) + (1,) * (len(shape) - position - 1))

    loudness = one(*pieces[0])
    for cut in pieces[1:]:
        loudness = loudness * one(*cut)
    return loudness


def noise(rng, extent, width, most, cuts=(), kind=jnp.bfloat16):
    values = width * jax.random.normal(rng, extent, jnp.float32)
    if cuts:
        values = values * block_levels(rng, extent, cuts, -0.22, 0.18)
    return jnp.clip(values, -most, most).astype(kind)


def setup_inputs(seed: int = 0) -> dict:
    seeds = jax.random.split(jax.random.key(seed), 12)
    chaos_modes = jnp.clip(jax.random.uniform(seeds[0], (P_SIZE, CELLS), jnp.float32, -0.2, 0.2) * block_levels(seeds[0], (P_SIZE, CELLS), ((1, 32),), -0.4, 0.0), -0.2, 0.2)
    newton_heading = jnp.clip(jax.random.uniform(seeds[1], (P_SIZE, CELLS), jnp.float32, -0.2, 0.2) * block_levels(seeds[1], (P_SIZE, CELLS), ((1, 32),), -0.4, 0.0), -0.2, 0.2)
    source = noise(seeds[2], (CELLS,), 1.0, 6.0, ((0, 32),), jnp.float32)
    nodes = noise(seeds[3], (Q, DIMS), 1.0, 3.0, (), jnp.float32)
    weights = jnp.clip(jax.random.uniform(seeds[4], (Q,), jnp.float32, 0.0009765625, 0.0029296875), 0.0009765625, 0.0029296875)
    k_ref = jnp.clip(jnp.exp(jax.random.uniform(seeds[5], (NMAT,), jnp.float32, math.log(0.5), math.log(4.0))), 0.5, 4.0)
    sensitivity = jnp.clip(jax.random.uniform(seeds[6], (NMAT, DIMS), jnp.float32, -0.1, 0.1), -0.1, 0.1)
    decay = jnp.clip(jnp.exp(jax.random.uniform(seeds[7], (NMAT,), jnp.float32, math.log(0.1), math.log(0.5))), 0.1, 0.5)
    material = place_ends(jax.random.randint(seeds[8], (N_SPACE * NB,), 0, NMAT), jax.random.fold_in(seeds[8], 1), 0, NMAT - 1).astype(jnp.int32)
    neighbors = draw_neighbors(jax.random.fold_in(seeds[11], 71), 0)
    send_list = draw_send_list(jax.random.fold_in(seeds[11], 71), 0)
    return dict(chaos_modes=chaos_modes, newton_heading=newton_heading, source=source, nodes=nodes, weights=weights, k_ref=k_ref, sensitivity=sensitivity, decay=decay, material=material, neighbors=neighbors, send_list=send_list)


lateral_factor = 0.5
cooler_multiplier = 2.0

def compositions(remaining, places):
    if places == 1:
        return [[remaining]]
    listing = []
    for leading in range(remaining, -1, -1):
        for trailing in compositions(remaining - leading, places - 1):
            listing.append([leading] + trailing)
    return listing

def chaos_orders(variables):
    listing = []
    for degree in range(4):
        listing = listing + compositions(degree, variables)
    return np.array(listing, dtype=np.int32)

def hermite_basis(points):
    polynomial_orders = chaos_orders(points.shape[1])
    scale_factors = np.array([1.0, 1.0, 1.0 / math.sqrt(2.0), 1.0 / math.sqrt(6.0)], dtype=np.float32)
    result = jnp.ones((points.shape[0], polynomial_orders.shape[0]), jnp.float32)
    for random_variable in range(points.shape[1]):
        column = points[:, random_variable]
        hermite = jnp.stack([jnp.ones_like(column), column, column * column - 1.0, column * column * column - 3.0 * column], axis=1)
        selection_mask = np.zeros((4, polynomial_orders.shape[0]), np.float32)
        selection_mask[polynomial_orders[:, random_variable], np.arange(polynomial_orders.shape[0])] = scale_factors[polynomial_orders[:, random_variable]]
        result = result * jnp.dot(hermite, jnp.asarray(selection_mask, dtype=jnp.float32), precision=lax.Precision.HIGHEST)
    return result

def pointwise_imbalance(site_kelvin, kelvin_linearized, diffusive_ability, admittance_linearized, interface_partner_slot):
    interface_transfer = 0.5 * (diffusive_ability[:, :, :-1] + diffusive_ability[:, :, 1:])
    interface_increment = 0.5 * (admittance_linearized[:, :, :-1] + admittance_linearized[:, :, 1:])
    kelvin_gap = site_kelvin[:, :, :-1] - site_kelvin[:, :, 1:]
    decline_increment = kelvin_linearized[:, :, :-1] - kelvin_linearized[:, :, 1:]
    heightwise_stream = interface_transfer * kelvin_gap
    stream_increment = interface_increment * kelvin_gap + interface_transfer * decline_increment
    padding_sheet = jnp.zeros(site_kelvin.shape[:2] + (1,), jnp.float32)
    energy_imbalance = jnp.concatenate([heightwise_stream, padding_sheet], 2) - jnp.concatenate([padding_sheet, heightwise_stream], 2)
    imbalance_linearized = jnp.concatenate([stream_increment, padding_sheet], 2) - jnp.concatenate([padding_sheet, stream_increment], 2)
    cooler_outflow = cooler_multiplier * diffusive_ability[:, :, :1] * site_kelvin[:, :, :1]
    cooler_linearized = cooler_multiplier * (admittance_linearized[:, :, :1] * site_kelvin[:, :, :1] + diffusive_ability[:, :, :1] * kelvin_linearized[:, :, :1])
    top_padding_sheet = jnp.zeros(site_kelvin.shape[:2] + (site_kelvin.shape[2] - 1,), jnp.float32)
    energy_imbalance = energy_imbalance + jnp.concatenate([cooler_outflow, top_padding_sheet], 2)
    imbalance_linearized = imbalance_linearized + jnp.concatenate([cooler_linearized, top_padding_sheet], 2)
    piled_vertical_lines = jnp.stack([site_kelvin, kelvin_linearized, diffusive_ability, admittance_linearized])
    for face_number in range(4):
        face_index = interface_partner_slot[:, face_number]
        present = (face_index >= 0).astype(jnp.float32)[None, :, None]
        bordering_sites = jnp.take(piled_vertical_lines, jnp.maximum(face_index, 0), axis=2)
        side_conduct = lateral_factor * 0.5 * (diffusive_ability + bordering_sites[2]) * present
        side_step = lateral_factor * 0.5 * (admittance_linearized + bordering_sites[3]) * present
        sideways_gap = site_kelvin - bordering_sites[0]
        flank_decline_increment = kelvin_linearized - bordering_sites[1]
        energy_imbalance = energy_imbalance + side_conduct * sideways_gap
        imbalance_linearized = imbalance_linearized + side_step * sideways_gap + side_conduct * flank_decline_increment
    return (energy_imbalance, imbalance_linearized)

def reference(chaos_modes, newton_heading, source, nodes, weights, k_ref, sensitivity, decay, material, neighbors, send_list):
    basis = hermite_basis(nodes)
    segment_aggregate = N_SPACE * NB
    owner_rank = jnp.arange(segment_aggregate, dtype=jnp.int32) // NB
    halo_ref = neighbors - NB
    peer_rank = jnp.clip(halo_ref // HMAX, 0, N_SPACE - 1).astype(jnp.int32)
    slot_index = jnp.clip(halo_ref % HMAX, 0, HMAX - 1).astype(jnp.int32)
    remote = send_list[peer_rank, owner_rank[:, None], slot_index]
    interface_partner_slot = jnp.where(neighbors < 0, -1, jnp.where(neighbors < NB, owner_rank[:, None] * NB + neighbors, peer_rank * NB + remote)).astype(jnp.int32)
    group_basis = basis.reshape(N_CHAOS, GAUSS_POINTS, basis.shape[1])
    group_weight = weights.reshape(N_CHAOS, GAUSS_POINTS)
    group_nodes = nodes.reshape(N_CHAOS, GAUSS_POINTS, nodes.shape[1])
    segment_damping = decay[material]

    def accumulate(totals, inputs):
        hermite_subset_evals, part_weight, part_nodes = inputs
        material_scale = k_ref[:, None] * jnp.exp(jnp.dot(sensitivity, part_nodes.T, precision=lax.Precision.HIGHEST))
        segment_multiplier = material_scale[material].T
        site_kelvin = jnp.dot(hermite_subset_evals, chaos_modes, precision=lax.Precision.HIGHEST).reshape(GAUSS_POINTS, segment_aggregate, SEGMENT_SITES)
        kelvin_linearized = jnp.dot(hermite_subset_evals, newton_heading, precision=lax.Precision.HIGHEST).reshape(GAUSS_POINTS, segment_aggregate, SEGMENT_SITES)
        diffusive_ability = segment_multiplier[:, :, None] * jnp.exp(-segment_damping[None, :, None] * site_kelvin)
        admittance_linearized = -segment_damping[None, :, None] * diffusive_ability * kelvin_linearized
        energy_imbalance, imbalance_linearized = pointwise_imbalance(site_kelvin, kelvin_linearized, diffusive_ability, admittance_linearized, interface_partner_slot)
        weighted = (energy_imbalance * part_weight[:, None, None]).reshape(GAUSS_POINTS, segment_aggregate * SEGMENT_SITES)
        weighted_step = (imbalance_linearized * part_weight[:, None, None]).reshape(GAUSS_POINTS, segment_aggregate * SEGMENT_SITES)
        first = totals[0] + jnp.dot(hermite_subset_evals.T, weighted, precision=lax.Precision.HIGHEST)
        second = totals[1] + jnp.dot(hermite_subset_evals.T, weighted_step, precision=lax.Precision.HIGHEST)
        return ((first, second), None)
    start = jnp.zeros(chaos_modes.shape, jnp.float32)
    (projected, projected_step), unused = lax.scan(accumulate, (start, start), (group_basis, group_weight, group_nodes))
    node_mass = jnp.dot(weights, basis, precision=lax.Precision.HIGHEST)
    residual = projected - node_mass[:, None] * source[None, :]
    return (residual, projected_step)
```

```python
import functools
import math

import jax
import jax.numpy as jnp
import numpy as np
from jax import lax
from jax.experimental import pallas as pl
from jax.experimental.pallas import tpu as pltpu
from jax.sharding import PartitionSpec as P

NMAT = 4
SITES = 64
TERMS = 84
MAIN = 80
LOG2E = 1.0 / math.log(2.0)
LN2 = math.log(2.0)
OFFSETS = (1, -1, 2, -2)
BF = jnp.bfloat16
F32 = jnp.float32


def compositions(remaining, places):
    if places == 1:
        return [[remaining]]
    listing = []
    for leading in range(remaining, -1, -1):
        for trailing in compositions(remaining - leading, places - 1):
            listing.append([leading] + trailing)
    return listing


def chaos_orders(variables):
    listing = []
    for degree in range(4):
        listing = listing + compositions(degree, variables)
    return np.array(listing, dtype=np.int32)


def products(nodes, orders, along):
    value = None
    for d in range(nodes.shape[1]):
        x = jnp.expand_dims(nodes[:, d], 1 - along)
        o = jnp.expand_dims(jnp.asarray(orders[:, d]), along)
        second = (x * x - 1.0) * np.float32(1.0 / math.sqrt(2.0))
        third = (x * x * x - 3.0 * x) * np.float32(1.0 / math.sqrt(6.0))
        factor = jnp.where(o == 0, 1.0, jnp.where(o == 1, x, jnp.where(o == 2, second, third)))
        value = factor if value is None else value * factor
    return value


def halves(x):
    high = lax.reduce_precision(x, 8, 7)
    return high, x - high


def tables(nodes, weights):
    orders = chaos_orders(nodes.shape[1])
    rest = np.arange(MAIN, TERMS)
    first = np.arange(MAIN)
    column = np.concatenate([first, first, first, rest, rest, rest, np.zeros(4, np.int64)])
    low = np.concatenate([np.zeros(160), np.ones(80), np.zeros(8), np.ones(4), np.zeros(4)])
    keep = np.concatenate([np.ones(252), np.zeros(4)])
    high, lower = halves(products(nodes, orders[column], 0))
    left = jnp.where(jnp.asarray(low[None, :] > 0), lower, high)
    left = jnp.where(jnp.asarray(keep[None, :] > 0), left, 0.0).astype(BF)
    back = np.concatenate([np.arange(TERMS), np.zeros(4, np.int64)])
    weighted = products(nodes, orders[back], 1) * weights[None, :]
    weighted = jnp.where(jnp.asarray(np.arange(88)[:, None] < TERMS), weighted, 0.0)
    high, lower = halves(weighted)
    right = jnp.concatenate([high, lower], 0).astype(BF)
    mass = jnp.sum(weighted, axis=1, keepdims=True)
    return left, right, mass


def place_rhs(rhs, face, field, main, tail):
    cols = slice(field * 128, field * 128 + 128)
    row = lax.broadcasted_iota(jnp.int32, (8, 128), 0)
    high = main.astype(BF)
    low = (main - high.astype(F32)).astype(BF)
    tail_high = tail.astype(BF).astype(F32)
    rhs[face, 0:80, cols] = high
    rhs[face, 80:160, cols] = low
    rhs[face, 160:240, cols] = high
    rhs[face, 240:256, cols] = jnp.concatenate(
        [
            jnp.where(row < 4, tail_high, tail - tail_high),
            jnp.where(row < 4, tail_high, 0.0),
        ],
        0,
    ).astype(BF)


def fields(x):
    row = lax.broadcasted_iota(jnp.int32, (8, 128), 0)
    mixed = x[160:168]
    turned = pltpu.roll(mixed, 4, 0)
    mode = (x[0:80], jnp.where(row < 4, mixed, turned))
    step = (x[80:160], jnp.where(row < 4, turned, mixed))
    aux = x[168:176]
    damp = aux[7:8]
    offset = jnp.where(row < 7, aux, 0.0)
    arg_main = mode[0] * damp
    arg_main = jnp.concatenate([arg_main[0:8] + offset, arg_main[8:80]], 0)
    arg = (arg_main, mode[1] * damp)
    rate = damp * LN2
    change = (step[0] * rate, step[1] * rate)
    return mode, step, arg, change


def pair_work(pair, base, ids, coefs, field, left, right, mass, source, res, jvp, rhs, kc, acc, own):
    lane = lax.broadcasted_iota(jnp.int32, (1, 128), 1)
    low_half = lane < 64
    height = lane % 64
    x = field[base + pair]
    mine = fields(x)
    place_rhs(rhs, 6, 0, *mine[2])
    place_rhs(rhs, 6, 1, *mine[3])
    for face in range(6):
        if face == 0:
            scale = jnp.where(height == 63, 0.0, 0.5)
            other = [tuple(pltpu.roll(a, 127, 1) for a in f) for f in mine]
            gap = [tuple((a - b) * scale for a, b in zip(mine[i], other[i])) for i in (0, 1)]
        elif face == 1:
            scale = jnp.where(height == 0, 1.0, 0.5)
            bottom = height == 0
            other = [tuple(pltpu.roll(a, 1, 1) for a in f) for f in mine]
            gap = [
                tuple((a - jnp.where(bottom, 0.0, b)) * scale for a, b in zip(mine[i], other[i]))
                for i in (0, 1)
            ]
            other = [
                tuple(jnp.where(bottom, a, b) for a, b in zip(mine[i], other[i])) for i in range(4)
            ]
        else:
            at = pair * 8 + (face - 2)
            e0 = ids[at]
            e1 = ids[at + 4]
            x0 = field[e0 // 2]
            x1 = field[e1 // 2]
            x0 = pltpu.roll(x0, (e0 % 2) * 64, 1)
            x1 = pltpu.roll(x1, (1 - e1 % 2) * 64, 1)
            scale = jnp.where(low_half, coefs[at], coefs[at + 4])
            other = fields(jnp.where(low_half, x0, x1))
            gap = [tuple((a - b) * scale for a, b in zip(mine[i], other[i])) for i in (0, 1)]
        place_rhs(rhs, face, 0, *gap[0])
        place_rhs(rhs, face, 1, *gap[1])
        place_rhs(rhs, face, 2, *other[2])
        place_rhs(rhs, face, 3, *other[3])
    total = None
    count = left.shape[0] // 512
    for part in range(count):
        rows = slice(part * 512, part * 512 + 512)
        basis = left[rows]
        r = jnp.dot(basis, rhs[6, :, 0:256], preferred_element_type=F32)
        conduct = jnp.exp2(r[:, 0:128])
        kc[0] = conduct
        kc[1] = conduct * r[:, 128:256]
        for face in range(6):
            r = jnp.dot(basis, rhs[face], preferred_element_type=F32)
            k = jnp.exp2(r[:, 256:384])
            a = kc[0] + k
            b = kc[1] + k * r[:, 384:512]
            gap = r[:, 0:128]
            bal = a * gap
            step = b * gap + a * r[:, 128:256]
            if face == 0:
                acc[0] = bal
                acc[1] = step
            else:
                acc[0] += bal
                acc[1] += step
        both = jnp.concatenate([acc[0], acc[1]], 1)
        high = both.astype(BF)
        low = (both - high.astype(F32)).astype(BF)
        w = right[:, rows]
        one = jnp.dot(w, high, preferred_element_type=F32)
        two = jnp.dot(w[0:88], low, preferred_element_type=F32)
        one = one[0:88] + one[88:176] + two
        total = one if total is None else total + one
    cols = pl.ds(pl.multiple_of(pair * 128, 128), 128)
    res[:, cols] = (total[:, 0:128] - mass[...] * source[:, cols])[0:TERMS]
    jvp[:, cols] = total[0:TERMS, 128:256]


def kernel(pairs, ids, coefs, start, field, left, right, mass, source, res, jvp, rhs, kc, acc):
    base = start[0]

    def body(pair, carry):
        pair_work(pair, base, ids, coefs, field, left, right, mass, source, res, jvp, rhs, kc, acc, None)
        return carry

    lax.fori_loop(0, pairs, body, 0)


def aux_rows(k_ref, sensitivity, decay, material):
    table = jnp.concatenate(
        [jnp.log(k_ref)[:, None], sensitivity, -decay[:, None]], axis=1
    ) * np.float32(LOG2E)
    mine = material.reshape(-1, 2)
    spread = jnp.repeat(mine, SITES, axis=1)[:, None, :]
    out = jnp.zeros((mine.shape[0], 8, 128), F32)
    for m in range(NMAT):
        out = jnp.where(spread == m, table[m][None, :, None], out)
    return out


def slots(neighbors, space_rank, space_count, chaos_rank, own_blocks, halo_depth):
    blocks = neighbors.shape[0]
    mine = lax.dynamic_slice_in_dim(neighbors, chaos_rank * own_blocks, own_blocks, 0)
    halo_ref = mine - blocks
    distance = (space_rank - halo_ref // halo_depth) % space_count
    order = jnp.where(
        distance == 1, 0, jnp.where(distance == space_count - 1, 1, jnp.where(distance == 2, 2, 3))
    )
    ids = jnp.where(mine >= blocks, blocks + order * halo_depth + halo_ref % halo_depth, mine)
    ids = jnp.maximum(ids, 0).reshape(-1)
    coefs = jnp.where(mine >= 0, 0.25, 0.0).astype(F32).reshape(-1)
    return ids, coefs


def per_device(
    chaos_modes, newton_heading, source, nodes, weights, k_ref, sensitivity, decay,
    material, neighbors, send_list,
):
    space_count = lax.axis_size("space")
    space_rank = lax.axis_index("space")
    chaos_rank = lax.axis_index("chaos")
    cells = chaos_modes.shape[1]
    pairs = cells // 128
    halo_depth = send_list.shape[2]
    packed = jnp.concatenate(
        [chaos_modes[:MAIN], newton_heading[:MAIN], chaos_modes[MAIN:], newton_heading[MAIN:]], 0
    )
    packed = packed.reshape(2 * TERMS, pairs, 128).transpose(1, 0, 2)
    everyone = lax.all_gather(packed, "chaos", axis=0, tiled=True)
    aux = aux_rows(k_ref, sensitivity, decay, material)
    local = jnp.concatenate([everyone, aux], axis=1)
    pieces = [local]
    for offset in OFFSETS:
        target = (space_rank + offset) % space_count
        rows = lax.dynamic_index_in_dim(send_list[0], target, 0, keepdims=False)
        picked = [
            lax.dynamic_slice(local, (rows[j] // 2, 0, (rows[j] % 2) * 64), (1, 176, 64))
            for j in range(halo_depth)
        ]
        outgoing = jnp.concatenate(picked, axis=2)
        pieces.append(
            lax.ppermute(
                outgoing, "space", [(i, (i + offset) % space_count) for i in range(space_count)]
            )
        )
    field = jnp.concatenate(pieces, axis=0)
    ids, coefs = slots(
        neighbors, space_rank, space_count, chaos_rank, cells // SITES, halo_depth
    )
    left, right, mass = tables(nodes, weights)
    start = (chaos_rank * pairs).astype(jnp.int32).reshape(1)
    vmem = pl.BlockSpec(memory_space=pltpu.VMEM)
    smem = pl.BlockSpec(memory_space=pltpu.SMEM)
    return pl.pallas_call(
        functools.partial(kernel, pairs),
        out_shape=[jax.ShapeDtypeStruct((TERMS, cells), F32)] * 2,
        in_specs=[smem, smem, smem, vmem, vmem, vmem, vmem, vmem],
        out_specs=[vmem, vmem],
        scratch_shapes=[
            pltpu.VMEM((7, 256, 512), BF),
            pltpu.VMEM((2, 512, 128), F32),
            pltpu.VMEM((2, 512, 128), F32),
        ],
        compiler_params=pltpu.CompilerParams(vmem_limit_bytes=48 * 1024 * 1024),
    )(ids, coefs, start, field, left, right, mass, source[None, :])


def solution(mesh):
    return jax.shard_map(
        per_device,
        mesh=mesh,
        in_specs=(
            P(None, ("space", "chaos")),
            P(None, ("space", "chaos")),
            P(("space", "chaos")),
            P(), P(), P(), P(), P(),
            P("space"),
            P("space", None),
            P("space", None, None),
        ),
        out_specs=(P(None, ("space", "chaos")), P(None, ("space", "chaos"))),
        check_vma=False,
    )
```

```python
import functools
import math

import jax
import jax.numpy as jnp
import numpy as np
from jax import lax
from jax.experimental import pallas as pl
from jax.experimental.pallas import tpu as pltpu
from jax.sharding import PartitionSpec as P

NMAT = 4
SITES = 64
TERMS = 84
MAIN = 80
LOG2E = 1.0 / math.log(2.0)
LN2 = math.log(2.0)
OFFSETS = (1, -1, 2, -2)
BF = jnp.bfloat16
F32 = jnp.float32


def compositions(remaining, places):
    if places == 1:
        return [[remaining]]
    listing = []
    for leading in range(remaining, -1, -1):
        for trailing in compositions(remaining - leading, places - 1):
            listing.append([leading] + trailing)
    return listing


def chaos_orders(variables):
    listing = []
    for degree in range(4):
        listing = listing + compositions(degree, variables)
    return np.array(listing, dtype=np.int32)


def half_turn(x, wanted):
    return jnp.where(wanted, pltpu.roll(x, 64, 1), x)


def factors(x, o):
    second = (x * x - 1.0) * np.float32(1.0 / math.sqrt(2.0))
    third = (x * x * x - 3.0 * x) * np.float32(1.0 / math.sqrt(6.0))
    return jnp.where(o == 0, 1.0, jnp.where(o == 1, x, jnp.where(o == 2, second, third)))


def order_tables(dims):
    orders = chaos_orders(dims)
    rest = np.arange(MAIN, TERMS)
    first = np.arange(MAIN)
    column = np.concatenate([first, first, first, rest, rest, rest, np.zeros(4, np.int64)])
    back = np.concatenate([np.arange(TERMS), np.zeros(4, np.int64)])
    return orders[column].T.copy(), orders[back].copy()


def fill_tables(nodes, nodes_t, weights, order_left, order_right, left, right, mass):
    dims = nodes.shape[1]
    column = lax.broadcasted_iota(jnp.int32, (1, 256), 1)
    lower = ((column >= 160) & (column < 240)) | ((column >= 248) & (column < 252))
    step = 128

    def body(part, carry):
        rows = pl.ds(pl.multiple_of(part * step, step), step)
        value = None
        for d in range(dims):
            f = factors(nodes[rows, d : d + 1], order_left[d : d + 1])
            value = f if value is None else value * f
        high = value.astype(BF).astype(F32)
        value = jnp.where(lower, value - high, high)
        left[rows] = jnp.where(column < 252, value, 0.0).astype(BF)
        return carry

    lax.fori_loop(0, nodes.shape[0] // step, body, 0)
    row = lax.broadcasted_iota(jnp.int32, (88, 1), 0)
    mass[...] = jnp.zeros(mass.shape, F32)

    def body_right(part, carry):
        cols = pl.ds(pl.multiple_of(part * step, step), step)
        value = weights[:, cols]
        for d in range(dims):
            value = value * factors(nodes_t[d : d + 1, cols], order_right[:, d : d + 1])
        value = jnp.where(row < TERMS, value, 0.0)
        high = value.astype(BF).astype(F32)
        right[:, cols] = jnp.concatenate([high, value - high], 0).astype(BF)
        mass[...] += jnp.sum(value, axis=1, keepdims=True)
        return carry

    lax.fori_loop(0, nodes.shape[0] // step, body_right, 0)


def remote(src, dst, send, recv, device):
    return pltpu.make_async_remote_copy(
        src_ref=src, dst_ref=dst, send_sem=send, recv_sem=recv,
        device_id=device, device_id_type=pl.DeviceIdType.MESH,
    )


def pack_own(modes, heading, pairs, base, field):
    for i in range(pairs):
        cols = slice(i * 128, i * 128 + 128)
        field[base + i, 0:80] = modes[0:80, cols]
        field[base + i, 80:160] = heading[0:80, cols]
        field[base + i, 160:168] = jnp.concatenate([modes[80:84, cols], heading[80:84, cols]], 0)


def greet(space_count, chaos_count, space, chaos):
    barrier = pltpu.get_barrier_semaphore()
    if chaos_count == 4:
        peers = [chaos + 1 - 2 * (chaos % 2), (chaos + 2) % 4]
    else:
        peers = [(chaos + k) % chaos_count for k in range(1, chaos_count)]
    for peer in peers:
        pl.semaphore_signal(
            barrier, inc=1, device_id={"chaos": peer}, device_id_type=pl.DeviceIdType.MESH
        )
    for offset in OFFSETS:
        pl.semaphore_signal(
            barrier, inc=1, device_id={"space": (space + offset + space_count) % space_count},
            device_id_type=pl.DeviceIdType.MESH,
        )
    pl.semaphore_wait(barrier, len(peers) + len(OFFSETS))
    return peers


def spread_modes(chaos_count, peers, chaos, pairs, field, send, recv, meanwhile):
    def block(owner, first, count):
        return field.at[pl.ds(owner * pairs + first, count), 0:168]

    if chaos_count == 4:
        across, along = peers
        half = pairs // 2
        plan = [
            (chaos, 0, across), (chaos, half, along),
            (chaos, half, across), (chaos, 0, along),
        ]
        copies = [
            remote(block(o, f, half), block(o, f, half), send.at[i], recv.at[i], {"chaos": t})
            for i, (o, f, t) in enumerate(plan)
        ]
        for copy in copies:
            copy.start()
        meanwhile()
        copies[0].wait_recv()
        on = remote(
            block(across, 0, half), block(across, 0, half), send.at[4], recv.at[4],
            {"chaos": along},
        )
        on.start()
        copies[1].wait_recv()
        over = remote(
            block(along, half, half), block(along, half, half), send.at[5], recv.at[5],
            {"chaos": across},
        )
        over.start()
        copies[2].wait_recv()
        copies[3].wait_recv()
        on.wait_recv()
        over.wait_recv()
        return copies + [on, over]
    copies = [
        remote(
            block(chaos, 0, pairs), block(chaos, 0, pairs), send.at[i], recv.at[i], {"chaos": t}
        )
        for i, t in enumerate(peers)
    ]
    for copy in copies:
        copy.start()
    meanwhile()
    for copy in copies:
        copy.wait_recv()
    return copies


def send_halo(space_count, space, picks, field, out, inbox, send, recv):
    low_half = lax.broadcasted_iota(jnp.int32, (1, 128), 1) < 64
    copies = []
    for i, offset in enumerate(OFFSETS):
        target = (space + offset + space_count) % space_count
        e0 = picks[2 * target]
        e1 = picks[2 * target + 1]
        x0 = half_turn(field[e0 // 2], e0 % 2 == 1)
        x1 = half_turn(field[e1 // 2], e1 % 2 == 0)
        out[i] = jnp.where(low_half, x0, x1)
        copy = remote(out.at[i], inbox.at[i], send.at[i], recv.at[i], {"space": target})
        copy.start()
        copies.append(copy)
    return copies


def gather_kernel(
    sizes, picks, modes, heading, aux, nodes, nodes_t, weights, order_left, order_right,
    field, left, right, mass, out, inbox, send, recv, halo_send, halo_recv,
):
    space_count, chaos_count, pairs = sizes
    space = lax.axis_index("space")
    chaos = lax.axis_index("chaos")
    blocks = aux.shape[0] * 2
    field[0 : blocks // 2, 168:176] = aux[...]
    pack_own(modes, heading, pairs, chaos * pairs, field)
    peers = greet(space_count, chaos_count, space, chaos)
    copies = spread_modes(
        chaos_count, peers, chaos, pairs, field, send, recv,
        lambda: fill_tables(
            nodes, nodes_t, weights, order_left, order_right, left, right, mass
        ),
    )
    halo = send_halo(space_count, space, picks, field, out, inbox, halo_send, halo_recv)
    for copy in copies:
        copy.wait_send()
    for i, copy in enumerate(halo):
        copy.wait()
        field[blocks // 2 + i] = inbox[i]


def place_rhs(rhs, face, field, main, tail):
    cols = slice(field * 128, field * 128 + 128)
    row = lax.broadcasted_iota(jnp.int32, (8, 128), 0)
    high = main.astype(BF)
    low = (main - high.astype(F32)).astype(BF)
    tail_high = tail.astype(BF).astype(F32)
    rhs[face, 0:80, cols] = high
    rhs[face, 80:160, cols] = low
    rhs[face, 160:240, cols] = high
    rhs[face, 240:256, cols] = jnp.concatenate(
        [
            jnp.where(row < 4, tail_high, tail - tail_high),
            jnp.where(row < 4, tail_high, 0.0),
        ],
        0,
    ).astype(BF)


def fields(x):
    row = lax.broadcasted_iota(jnp.int32, (8, 128), 0)
    mixed = x[160:168]
    turned = pltpu.roll(mixed, 4, 0)
    mode = (x[0:80], jnp.where(row < 4, mixed, turned))
    step = (x[80:160], jnp.where(row < 4, turned, mixed))
    aux = x[168:176]
    damp = aux[7:8]
    offset = jnp.where(row < 7, aux, 0.0)
    arg_main = mode[0] * damp
    arg_main = jnp.concatenate([arg_main[0:8] + offset, arg_main[8:80]], 0)
    arg = (arg_main, mode[1] * damp)
    rate = damp * LN2
    change = (step[0] * rate, step[1] * rate)
    return mode, step, arg, change


def pair_work(pair, base, ids, coefs, field, left, right, mass, source, res, jvp, rhs, kc, acc, own):
    lane = lax.broadcasted_iota(jnp.int32, (1, 128), 1)
    low_half = lane < 64
    height = lane % 64
    x = field[base + pair]
    mine = fields(x)
    place_rhs(rhs, 6, 0, *mine[2])
    place_rhs(rhs, 6, 1, *mine[3])
    for face in range(6):
        if face == 0:
            scale = jnp.where(height == 63, 0.0, 0.5)
            other = [tuple(pltpu.roll(a, 127, 1) for a in f) for f in mine]
            gap = [tuple((a - b) * scale for a, b in zip(mine[i], other[i])) for i in (0, 1)]
        elif face == 1:
            scale = jnp.where(height == 0, 1.0, 0.5)
            bottom = height == 0
            other = [tuple(pltpu.roll(a, 1, 1) for a in f) for f in mine]
            gap = [
                tuple((a - jnp.where(bottom, 0.0, b)) * scale for a, b in zip(mine[i], other[i]))
                for i in (0, 1)
            ]
            other = [
                tuple(jnp.where(bottom, a, b) for a, b in zip(mine[i], other[i])) for i in range(4)
            ]
        else:
            at = pair * 8 + (face - 2)
            e0 = ids[at]
            e1 = ids[at + 4]
            x0 = half_turn(field[e0 // 2], e0 % 2 == 1)
            x1 = half_turn(field[e1 // 2], e1 % 2 == 0)
            scale = jnp.where(low_half, coefs[at], coefs[at + 4])
            other = fields(jnp.where(low_half, x0, x1))
            gap = [tuple((a - b) * scale for a, b in zip(mine[i], other[i])) for i in (0, 1)]
        place_rhs(rhs, face, 0, *gap[0])
        place_rhs(rhs, face, 1, *gap[1])
        place_rhs(rhs, face, 2, *other[2])
        place_rhs(rhs, face, 3, *other[3])
    total = None
    count = left.shape[0] // 512
    for part in range(count):
        rows = slice(part * 512, part * 512 + 512)
        basis = left[rows]
        r = jnp.dot(basis, rhs[6, :, 0:256], preferred_element_type=F32)
        conduct = jnp.exp2(r[:, 0:128])
        kc[0] = conduct
        kc[1] = conduct * r[:, 128:256]
        for face in range(6):
            r = jnp.dot(basis, rhs[face], preferred_element_type=F32)
            k = jnp.exp2(r[:, 256:384])
            a = kc[0] + k
            b = kc[1] + k * r[:, 384:512]
            gap = r[:, 0:128]
            bal = a * gap
            step = b * gap + a * r[:, 128:256]
            if face == 0:
                acc[0] = bal
                acc[1] = step
            else:
                acc[0] += bal
                acc[1] += step
        both = jnp.concatenate([acc[0], acc[1]], 1)
        high = both.astype(BF)
        low = (both - high.astype(F32)).astype(BF)
        w = right[:, rows]
        one = jnp.dot(w, high, preferred_element_type=F32)
        two = jnp.dot(w[0:88], low, preferred_element_type=F32)
        one = one[0:88] + one[88:176] + two
        total = one if total is None else total + one
    cols = pl.ds(pl.multiple_of(pair * 128, 128), 128)
    res[:, cols] = (total[:, 0:128] - mass[...] * source[:, cols])[0:TERMS]
    jvp[:, cols] = total[0:TERMS, 128:256]


def kernel(pairs, ids, coefs, start, field, left, right, mass, source, res, jvp, rhs, kc, acc):
    base = start[0]

    def body(pair, carry):
        pair_work(pair, base, ids, coefs, field, left, right, mass, source, res, jvp, rhs, kc, acc, None)
        return carry

    lax.fori_loop(0, pairs, body, 0)


def aux_rows(k_ref, sensitivity, decay, material):
    table = jnp.concatenate(
        [jnp.log(k_ref)[:, None], sensitivity, -decay[:, None]], axis=1
    ) * np.float32(LOG2E)
    mine = material.reshape(-1, 2)
    spread = jnp.repeat(mine, SITES, axis=1)[:, None, :]
    out = jnp.zeros((mine.shape[0], 8, 128), F32)
    for m in range(NMAT):
        out = jnp.where(spread == m, table[m][None, :, None], out)
    return out


def slots(neighbors, space_rank, space_count, chaos_rank, own_blocks, halo_depth):
    blocks = neighbors.shape[0]
    mine = lax.dynamic_slice_in_dim(neighbors, chaos_rank * own_blocks, own_blocks, 0)
    halo_ref = mine - blocks
    distance = (space_rank - halo_ref // halo_depth) % space_count
    order = jnp.where(
        distance == 1, 0, jnp.where(distance == space_count - 1, 1, jnp.where(distance == 2, 2, 3))
    )
    ids = jnp.where(mine >= blocks, blocks + order * halo_depth + halo_ref % halo_depth, mine)
    ids = jnp.maximum(ids, 0).reshape(-1)
    coefs = jnp.where(mine >= 0, 0.25, 0.0).astype(F32).reshape(-1)
    return ids, coefs


def per_device(
    chaos_modes, newton_heading, source, nodes, weights, k_ref, sensitivity, decay,
    material, neighbors, send_list,
):
    space_count = lax.axis_size("space")
    space_rank = lax.axis_index("space")
    chaos_rank = lax.axis_index("chaos")
    cells = chaos_modes.shape[1]
    pairs = cells // 128
    halo_depth = send_list.shape[2]
    queue = nodes.shape[0]
    blocks = material.shape[0]
    aux = aux_rows(k_ref, sensitivity, decay, material)
    order_left, order_right = order_tables(nodes.shape[1])
    vmem = pl.BlockSpec(memory_space=pltpu.VMEM)
    smem = pl.BlockSpec(memory_space=pltpu.SMEM)
    field, left, right, mass = pl.pallas_call(
        functools.partial(gather_kernel, (space_count, lax.axis_size("chaos"), pairs)),
        out_shape=[
            jax.ShapeDtypeStruct((blocks // 2 + 4, 176, 128), F32),
            jax.ShapeDtypeStruct((queue, 256), BF),
            jax.ShapeDtypeStruct((176, queue), BF),
            jax.ShapeDtypeStruct((88, 1), F32),
        ],
        in_specs=[smem] + [vmem] * 8,
        out_specs=[vmem] * 4,
        scratch_shapes=[
            pltpu.VMEM((4, 176, 128), F32),
            pltpu.VMEM((4, 176, 128), F32),
            pltpu.SemaphoreType.DMA((16,)),
            pltpu.SemaphoreType.DMA((16,)),
            pltpu.SemaphoreType.DMA((4,)),
            pltpu.SemaphoreType.DMA((4,)),
        ],
        compiler_params=pltpu.CompilerParams(
            collective_id=0, has_side_effects=True, vmem_limit_bytes=32 * 1024 * 1024
        ),
    )(
        send_list.reshape(-1), chaos_modes, newton_heading, aux, nodes, nodes.T,
        weights[None, :], jnp.asarray(order_left), jnp.asarray(order_right),
    )
    ids, coefs = slots(
        neighbors, space_rank, space_count, chaos_rank, cells // SITES, halo_depth
    )
    start = (chaos_rank * pairs).astype(jnp.int32).reshape(1)
    return pl.pallas_call(
        functools.partial(kernel, pairs),
        out_shape=[jax.ShapeDtypeStruct((TERMS, cells), F32)] * 2,
        in_specs=[smem, smem, smem, vmem, vmem, vmem, vmem, vmem],
        out_specs=[vmem, vmem],
        scratch_shapes=[
            pltpu.VMEM((7, 256, 512), BF),
            pltpu.VMEM((2, 512, 128), F32),
            pltpu.VMEM((2, 512, 128), F32),
        ],
        compiler_params=pltpu.CompilerParams(vmem_limit_bytes=48 * 1024 * 1024),
    )(ids, coefs, start, field, left, right, mass, source[None, :])


def solution(mesh):
    return jax.shard_map(
        per_device,
        mesh=mesh,
        in_specs=(
            P(None, ("space", "chaos")),
            P(None, ("space", "chaos")),
            P(("space", "chaos")),
            P(), P(), P(), P(), P(),
            P("space"),
            P("space", None),
            P("space", None, None),
        ),
        out_specs=(P(None, ("space", "chaos")), P(None, ("space", "chaos"))),
        check_vma=False,
    )
```

```python
import functools
import math

import jax
import jax.numpy as jnp
import numpy as np
from jax import lax
from jax.experimental import pallas as pl
from jax.experimental.pallas import tpu as pltpu
from jax.sharding import PartitionSpec as P

NMAT = 4
SITES = 64
TERMS = 84
MAIN = 80
LOG2E = 1.0 / math.log(2.0)
LN2 = math.log(2.0)
OFFSETS = (1, -1, 2, -2)
BF = jnp.bfloat16
F32 = jnp.float32


def compositions(remaining, places):
    if places == 1:
        return [[remaining]]
    listing = []
    for leading in range(remaining, -1, -1):
        for trailing in compositions(remaining - leading, places - 1):
            listing.append([leading] + trailing)
    return listing


def chaos_orders(variables):
    listing = []
    for degree in range(4):
        listing = listing + compositions(degree, variables)
    return np.array(listing, dtype=np.int32)


def half_turn(x, wanted):
    return jnp.where(wanted, pltpu.roll(x, 64, 1), x)


def factors(x, o):
    second = (x * x - 1.0) * np.float32(1.0 / math.sqrt(2.0))
    third = (x * x * x - 3.0 * x) * np.float32(1.0 / math.sqrt(6.0))
    return jnp.where(o == 0, 1.0, jnp.where(o == 1, x, jnp.where(o == 2, second, third)))


def order_codes(dims):
    orders = chaos_orders(dims)
    code = (orders * 4 ** np.arange(dims)[None, :]).sum(1)
    rest = np.arange(MAIN, TERMS)
    first = np.arange(MAIN)
    column = np.concatenate([first, first, first, rest, rest, rest, np.zeros(4, np.int64)])
    out = np.zeros((8, 256), np.float32)
    out[0] = code[column]
    out[1, :TERMS] = code
    return out


def upright(row):
    return jnp.transpose(jnp.broadcast_to(row, (128, 128)))


def fill_tables(nodes_t, weights, codes, left, right, mass):
    dims = nodes_t.shape[0]
    column = lax.broadcasted_iota(jnp.int32, (1, 128), 1)
    code_right = upright(codes[1:2, 0:128])[0:88].astype(jnp.int32)
    row = lax.broadcasted_iota(jnp.int32, (88, 1), 0)
    mass[...] = jnp.zeros(mass.shape, F32)

    def body(part, carry):
        span = pl.ds(pl.multiple_of(part * 128, 128), 128)
        points = [nodes_t[d : d + 1, span] for d in range(dims)]
        stood = [upright(x) for x in points]
        for side in range(2):
            code = codes[0:1, side * 128 : side * 128 + 128].astype(jnp.int32)
            at = column + side * 128
            lower = ((at >= 160) & (at < 240)) | ((at >= 248) & (at < 252))
            value = None
            for d in range(dims):
                f = factors(stood[d], (code // 4**d) % 4)
                value = f if value is None else value * f
            high = value.astype(BF).astype(F32)
            value = jnp.where(lower, value - high, high)
            left[span, side * 128 : side * 128 + 128] = jnp.where(at < 252, value, 0.0).astype(BF)
        value = weights[:, span]
        for d in range(dims):
            value = value * factors(points[d], (code_right // 4**d) % 4)
        value = jnp.where(row < TERMS, value, 0.0)
        high = value.astype(BF).astype(F32)
        right[:, span] = jnp.concatenate([high, value - high], 0).astype(BF)
        mass[...] += jnp.sum(value, axis=1, keepdims=True)
        return carry

    lax.fori_loop(0, nodes_t.shape[1] // 128, body, 0)


def fill_aux(k_ref, sensitivity, decay, material, table, field):
    row = lax.broadcasted_iota(jnp.int32, (8, 128), 0)
    low_half = lax.broadcasted_iota(jnp.int32, (8, 128), 1) < 64
    dims = sensitivity.shape[1]
    for m in range(NMAT):
        tile = jnp.log(jnp.full((8, 128), k_ref[m], F32))
        for d in range(dims):
            tile = jnp.where(row == d + 1, sensitivity[m, d], tile)
        tile = jnp.where(row == 7, -decay[m], tile)
        table[m] = tile * np.float32(LOG2E)
    for i in range(material.shape[0] // 2):
        field[i, 168:176] = jnp.where(low_half, table[material[2 * i]], table[material[2 * i + 1]])


def remote(src, dst, send, recv, device):
    return pltpu.make_async_remote_copy(
        src_ref=src, dst_ref=dst, send_sem=send, recv_sem=recv,
        device_id=device, device_id_type=pl.DeviceIdType.MESH,
    )


def pack_own(modes, heading, pairs, base, field):
    for i in range(pairs):
        cols = slice(i * 128, i * 128 + 128)
        field[base + i, 0:80] = modes[0:80, cols]
        field[base + i, 80:160] = heading[0:80, cols]
        field[base + i, 160:168] = jnp.concatenate([modes[80:84, cols], heading[80:84, cols]], 0)


def greet(space_count, chaos_count, space, chaos):
    barrier = pltpu.get_barrier_semaphore()
    if chaos_count == 4:
        peers = [chaos + 1 - 2 * (chaos % 2), (chaos + 2) % 4]
    else:
        peers = [(chaos + k) % chaos_count for k in range(1, chaos_count)]
    for peer in peers:
        pl.semaphore_signal(
            barrier, inc=1, device_id={"chaos": peer}, device_id_type=pl.DeviceIdType.MESH
        )
    for offset in OFFSETS:
        pl.semaphore_signal(
            barrier, inc=1, device_id={"space": (space + offset + space_count) % space_count},
            device_id_type=pl.DeviceIdType.MESH,
        )
    pl.semaphore_wait(barrier, len(peers) + len(OFFSETS))
    return peers


def spread_modes(chaos_count, peers, chaos, pairs, field, send, recv, meanwhile):
    def block(owner, first, count):
        return field.at[pl.ds(owner * pairs + first, count), 0:168]

    if chaos_count == 4:
        across, along = peers
        half = pairs // 2
        plan = [
            (chaos, 0, across), (chaos, half, along),
            (chaos, half, across), (chaos, 0, along),
        ]
        copies = [
            remote(block(o, f, half), block(o, f, half), send.at[i], recv.at[i], {"chaos": t})
            for i, (o, f, t) in enumerate(plan)
        ]
        for copy in copies:
            copy.start()
        meanwhile()
        copies[0].wait_recv()
        on = remote(
            block(across, 0, half), block(across, 0, half), send.at[4], recv.at[4],
            {"chaos": along},
        )
        on.start()
        copies[1].wait_recv()
        over = remote(
            block(along, half, half), block(along, half, half), send.at[5], recv.at[5],
            {"chaos": across},
        )
        over.start()
        copies[2].wait_recv()
        copies[3].wait_recv()
        on.wait_recv()
        over.wait_recv()
        return copies + [on, over]
    copies = [
        remote(
            block(chaos, 0, pairs), block(chaos, 0, pairs), send.at[i], recv.at[i], {"chaos": t}
        )
        for i, t in enumerate(peers)
    ]
    for copy in copies:
        copy.start()
    meanwhile()
    for copy in copies:
        copy.wait_recv()
    return copies


def send_halo(space_count, space, picks, field, out, inbox, send, recv):
    low_half = lax.broadcasted_iota(jnp.int32, (1, 128), 1) < 64
    copies = []
    for i, offset in enumerate(OFFSETS):
        target = (space + offset + space_count) % space_count
        e0 = picks[2 * target]
        e1 = picks[2 * target + 1]
        x0 = half_turn(field[e0 // 2], e0 % 2 == 1)
        x1 = half_turn(field[e1 // 2], e1 % 2 == 0)
        out[i] = jnp.where(low_half, x0, x1)
        copy = remote(out.at[i], inbox.at[i], send.at[i], recv.at[i], {"space": target})
        copy.start()
        copies.append(copy)
    return copies


def gather_kernel(
    sizes, picks, k_ref, sensitivity, decay, material, modes_far, heading_far, nodes_far,
    weights_far, codes_far, field, left, right, mass,
    modes, heading, nodes_t, weights, codes, table, out, inbox,
    send, recv, halo_send, halo_recv, near,
):
    space_count, chaos_count, pairs = sizes
    space = lax.axis_index("space")
    chaos = lax.axis_index("chaos")
    blocks = material.shape[0]
    loads = [
        pltpu.make_async_copy(a, b, near.at[i])
        for i, (a, b) in enumerate(
            [
                (modes_far, modes), (heading_far, heading), (nodes_far, nodes_t),
                (weights_far, weights), (codes_far, codes),
            ]
        )
    ]
    for load in loads:
        load.start()
    fill_aux(k_ref, sensitivity, decay, material, table, field)
    for load in loads:
        load.wait()
    pack_own(modes, heading, pairs, chaos * pairs, field)
    peers = greet(space_count, chaos_count, space, chaos)
    copies = spread_modes(
        chaos_count, peers, chaos, pairs, field, send, recv,
        lambda: fill_tables(nodes_t, weights, codes, left, right, mass),
    )
    halo = send_halo(space_count, space, picks, field, out, inbox, halo_send, halo_recv)
    for copy in copies:
        copy.wait_send()
    for i, copy in enumerate(halo):
        copy.wait()
        field[blocks // 2 + i] = inbox[i]


def place_rhs(rhs, face, field, main, tail):
    cols = slice(field * 128, field * 128 + 128)
    row = lax.broadcasted_iota(jnp.int32, (8, 128), 0)
    high = main.astype(BF)
    low = (main - high.astype(F32)).astype(BF)
    tail_high = tail.astype(BF).astype(F32)
    rhs[face, 0:80, cols] = high
    rhs[face, 80:160, cols] = low
    rhs[face, 160:240, cols] = high
    rhs[face, 240:256, cols] = jnp.concatenate(
        [
            jnp.where(row < 4, tail_high, tail - tail_high),
            jnp.where(row < 4, tail_high, 0.0),
        ],
        0,
    ).astype(BF)


def fields(x):
    row = lax.broadcasted_iota(jnp.int32, (8, 128), 0)
    mixed = x[160:168]
    turned = pltpu.roll(mixed, 4, 0)
    mode = (x[0:80], jnp.where(row < 4, mixed, turned))
    step = (x[80:160], jnp.where(row < 4, turned, mixed))
    aux = x[168:176]
    damp = aux[7:8]
    offset = jnp.where(row < 7, aux, 0.0)
    arg_main = mode[0] * damp
    arg_main = jnp.concatenate([arg_main[0:8] + offset, arg_main[8:80]], 0)
    arg = (arg_main, mode[1] * damp)
    rate = damp * LN2
    change = (step[0] * rate, step[1] * rate)
    return mode, step, arg, change


def slot(neighbors, block, face, ranks, halo_depth):
    space, space_count, blocks = ranks
    entry = neighbors[block, face]
    away = jnp.maximum(entry - blocks, 0)
    distance = (space - away // halo_depth + space_count) % space_count
    order = jnp.where(
        distance == 1, 0, jnp.where(distance == space_count - 1, 1, jnp.where(distance == 2, 2, 3))
    )
    index = jnp.where(
        entry >= blocks, blocks + order * halo_depth + away % halo_depth, jnp.maximum(entry, 0)
    )
    return index, jnp.where(entry >= 0, np.float32(0.25), np.float32(0.0))


def pair_work(
    pair, base, ranks, halo_depth, neighbors, field, left, right, mass, source, res, jvp, rhs,
    kc, acc,
):
    lane = lax.broadcasted_iota(jnp.int32, (1, 128), 1)
    low_half = lane < 64
    height = lane % 64
    x = field[base + pair]
    mine = fields(x)
    place_rhs(rhs, 6, 0, *mine[2])
    place_rhs(rhs, 6, 1, *mine[3])
    for face in range(6):
        if face == 0:
            scale = jnp.where(height == 63, 0.0, 0.5)
            other = [tuple(pltpu.roll(a, 127, 1) for a in f) for f in mine]
            gap = [tuple((a - b) * scale for a, b in zip(mine[i], other[i])) for i in (0, 1)]
        elif face == 1:
            scale = jnp.where(height == 0, 1.0, 0.5)
            bottom = height == 0
            other = [tuple(pltpu.roll(a, 1, 1) for a in f) for f in mine]
            gap = [
                tuple((a - jnp.where(bottom, 0.0, b)) * scale for a, b in zip(mine[i], other[i]))
                for i in (0, 1)
            ]
            other = [
                tuple(jnp.where(bottom, a, b) for a, b in zip(mine[i], other[i])) for i in range(4)
            ]
        else:
            e0, c0 = slot(neighbors, 2 * (base + pair), face - 2, ranks, halo_depth)
            e1, c1 = slot(neighbors, 2 * (base + pair) + 1, face - 2, ranks, halo_depth)
            x0 = half_turn(field[e0 // 2], e0 % 2 == 1)
            x1 = half_turn(field[e1 // 2], e1 % 2 == 0)
            scale = jnp.where(low_half, c0, c1)
            other = fields(jnp.where(low_half, x0, x1))
            gap = [tuple((a - b) * scale for a, b in zip(mine[i], other[i])) for i in (0, 1)]
        place_rhs(rhs, face, 0, *gap[0])
        place_rhs(rhs, face, 1, *gap[1])
        place_rhs(rhs, face, 2, *other[2])
        place_rhs(rhs, face, 3, *other[3])
    total = None
    count = left.shape[0] // 512
    for part in range(count):
        rows = slice(part * 512, part * 512 + 512)
        basis = left[rows]
        r = jnp.dot(basis, rhs[6, :, 0:256], preferred_element_type=F32)
        conduct = jnp.exp2(r[:, 0:128])
        kc[0] = conduct
        kc[1] = conduct * r[:, 128:256]
        for face in range(6):
            r = jnp.dot(basis, rhs[face], preferred_element_type=F32)
            k = jnp.exp2(r[:, 256:384])
            a = kc[0] + k
            b = kc[1] + k * r[:, 384:512]
            gap = r[:, 0:128]
            bal = a * gap
            step = b * gap + a * r[:, 128:256]
            if face == 0:
                acc[0] = bal
                acc[1] = step
            else:
                acc[0] += bal
                acc[1] += step
        both = jnp.concatenate([acc[0], acc[1]], 1)
        high = both.astype(BF)
        low = (both - high.astype(F32)).astype(BF)
        w = right[:, rows]
        one = jnp.dot(w, high, preferred_element_type=F32)
        two = jnp.dot(w[0:88], low, preferred_element_type=F32)
        one = one[0:88] + one[88:176] + two
        total = one if total is None else total + one
    cols = pl.ds(pl.multiple_of(pair * 128, 128), 128)
    res[:, cols] = (total[:, 0:128] - mass[...] * source[:, cols])[0:TERMS]
    jvp[:, cols] = total[0:TERMS, 128:256]


def kernel(
    pairs, space_count, halo_depth, neighbors, field, left, right, mass, source, res, jvp, rhs,
    kc, acc,
):
    base = lax.axis_index("chaos") * pairs
    ranks = (lax.axis_index("space"), space_count, neighbors.shape[0])

    def body(pair, carry):
        pair_work(
            pair, base, ranks, halo_depth, neighbors, field, left, right, mass, source, res,
            jvp, rhs, kc, acc,
        )
        return carry

    lax.fori_loop(0, pairs, body, 0)


def per_device(
    chaos_modes, newton_heading, source, nodes, weights, k_ref, sensitivity, decay,
    material, neighbors, send_list,
):
    space_count = lax.axis_size("space")
    cells = chaos_modes.shape[1]
    pairs = cells // 128
    halo_depth = send_list.shape[2]
    queue = nodes.shape[0]
    blocks = material.shape[0]
    far = pl.BlockSpec(memory_space=pl.ANY)
    vmem = pl.BlockSpec(memory_space=pltpu.VMEM)
    smem = pl.BlockSpec(memory_space=pltpu.SMEM)
    field, left, right, mass = pl.pallas_call(
        functools.partial(gather_kernel, (space_count, lax.axis_size("chaos"), pairs)),
        out_shape=[
            jax.ShapeDtypeStruct((blocks // 2 + 4, 176, 128), F32),
            jax.ShapeDtypeStruct((queue, 256), BF),
            jax.ShapeDtypeStruct((176, queue), BF),
            jax.ShapeDtypeStruct((88, 1), F32),
        ],
        in_specs=[smem] * 5 + [far] * 5,
        out_specs=[vmem] * 4,
        scratch_shapes=[
            pltpu.VMEM((TERMS, cells), F32),
            pltpu.VMEM((TERMS, cells), F32),
            pltpu.VMEM((nodes.shape[1], queue), F32),
            pltpu.VMEM((1, queue), F32),
            pltpu.VMEM((8, 256), F32),
            pltpu.VMEM((NMAT, 8, 128), F32),
            pltpu.VMEM((4, 176, 128), F32),
            pltpu.VMEM((4, 176, 128), F32),
            pltpu.SemaphoreType.DMA((16,)),
            pltpu.SemaphoreType.DMA((16,)),
            pltpu.SemaphoreType.DMA((4,)),
            pltpu.SemaphoreType.DMA((4,)),
            pltpu.SemaphoreType.DMA((5,)),
        ],
        compiler_params=pltpu.CompilerParams(
            collective_id=0, has_side_effects=True, vmem_limit_bytes=32 * 1024 * 1024
        ),
    )(
        send_list.reshape(-1), k_ref, sensitivity, decay, material, chaos_modes, newton_heading,
        nodes.T, weights[None, :], jnp.asarray(order_codes(nodes.shape[1])),
    )
    return pl.pallas_call(
        functools.partial(kernel, pairs, space_count, halo_depth),
        out_shape=[jax.ShapeDtypeStruct((TERMS, cells), F32)] * 2,
        in_specs=[smem, vmem, vmem, vmem, vmem, vmem],
        out_specs=[vmem, vmem],
        scratch_shapes=[
            pltpu.VMEM((7, 256, 512), BF),
            pltpu.VMEM((2, 512, 128), F32),
            pltpu.VMEM((2, 512, 128), F32),
        ],
        compiler_params=pltpu.CompilerParams(vmem_limit_bytes=48 * 1024 * 1024),
    )(neighbors, field, left, right, mass, source[None, :])


def solution(mesh):
    return jax.shard_map(
        per_device,
        mesh=mesh,
        in_specs=(
            P(None, ("space", "chaos")),
            P(None, ("space", "chaos")),
            P(("space", "chaos")),
            P(), P(), P(), P(), P(),
            P("space"),
            P("space", None),
            P("space", None, None),
        ),
        out_specs=(P(None, ("space", "chaos")), P(None, ("space", "chaos"))),
        check_vma=False,
    )
```

```python
import functools
import math

import jax
import jax.numpy as jnp
import numpy as np
from jax import lax
from jax.experimental import pallas as pl
from jax.experimental.pallas import tpu as pltpu
from jax.sharding import PartitionSpec as P

NMAT = 4
SITES = 64
TERMS = 84
MAIN = 80
LOG2E = 1.0 / math.log(2.0)
LN2 = math.log(2.0)
OFFSETS = (1, -1, 2, -2)
BF = jnp.bfloat16
F32 = jnp.float32


def compositions(remaining, places):
    if places == 1:
        return [[remaining]]
    listing = []
    for leading in range(remaining, -1, -1):
        for trailing in compositions(remaining - leading, places - 1):
            listing.append([leading] + trailing)
    return listing


def chaos_orders(variables):
    listing = []
    for degree in range(4):
        listing = listing + compositions(degree, variables)
    return np.array(listing, dtype=np.int32)


def half_turn(x, wanted):
    return jnp.where(wanted, pltpu.roll(x, 64, 1), x)


def factors(x, o):
    second = (x * x - 1.0) * np.float32(1.0 / math.sqrt(2.0))
    third = (x * x * x - 3.0 * x) * np.float32(1.0 / math.sqrt(6.0))
    return jnp.where(o == 0, 1.0, jnp.where(o == 1, x, jnp.where(o == 2, second, third)))


def order_codes(dims):
    orders = chaos_orders(dims)
    code = (orders * 4 ** np.arange(dims)[None, :]).sum(1)
    rest = np.arange(MAIN, TERMS)
    first = np.arange(MAIN)
    column = np.concatenate([first, first, first, rest, rest, rest, np.zeros(4, np.int64)])
    out = np.zeros((8, 256), np.float32)
    out[0] = code[column]
    out[1, :TERMS] = code
    return out


def upright(row):
    return jnp.transpose(jnp.broadcast_to(row, (128, 128)))


def fill_tables(nodes_t, weights, codes, left, right, mass):
    dims = nodes_t.shape[0]
    column = lax.broadcasted_iota(jnp.int32, (1, 128), 1)
    code_right = upright(codes[1:2, 0:128])[0:88].astype(jnp.int32)
    row = lax.broadcasted_iota(jnp.int32, (88, 1), 0)
    mass[...] = jnp.zeros(mass.shape, F32)

    def body(part, carry):
        span = pl.ds(pl.multiple_of(part * 128, 128), 128)
        points = [nodes_t[d : d + 1, span] for d in range(dims)]
        stood = [upright(x) for x in points]
        for side in range(2):
            code = codes[0:1, side * 128 : side * 128 + 128].astype(jnp.int32)
            at = column + side * 128
            lower = ((at >= 160) & (at < 240)) | ((at >= 248) & (at < 252))
            value = None
            for d in range(dims):
                f = factors(stood[d], (code // 4**d) % 4)
                value = f if value is None else value * f
            high = value.astype(BF).astype(F32)
            value = jnp.where(lower, value - high, high)
            left[span, side * 128 : side * 128 + 128] = jnp.where(at < 252, value, 0.0).astype(BF)
        value = weights[:, span]
        for d in range(dims):
            value = value * factors(points[d], (code_right // 4**d) % 4)
        value = jnp.where(row < TERMS, value, 0.0)
        high = value.astype(BF).astype(F32)
        right[:, span] = jnp.concatenate([high, value - high], 0).astype(BF)
        mass[...] += jnp.sum(value, axis=1, keepdims=True)
        return carry

    lax.fori_loop(0, nodes_t.shape[1] // 128, body, 0)


def fill_aux(k_ref, sensitivity, decay, material, table, field):
    row = lax.broadcasted_iota(jnp.int32, (8, 128), 0)
    low_half = lax.broadcasted_iota(jnp.int32, (8, 128), 1) < 64
    dims = sensitivity.shape[1]
    for m in range(NMAT):
        tile = jnp.log(jnp.full((8, 128), k_ref[m], F32))
        for d in range(dims):
            tile = jnp.where(row == d + 1, sensitivity[m, d], tile)
        tile = jnp.where(row == 7, -decay[m], tile)
        table[m] = tile * np.float32(LOG2E)
    for i in range(material.shape[0] // 2):
        field[i, 168:176] = jnp.where(low_half, table[material[2 * i]], table[material[2 * i + 1]])


def remote(src, dst, send, recv, device):
    return pltpu.make_async_remote_copy(
        src_ref=src, dst_ref=dst, send_sem=send, recv_sem=recv,
        device_id=device, device_id_type=pl.DeviceIdType.MESH,
    )


def pack_own(modes, heading, pairs, base, field):
    for i in range(pairs):
        cols = slice(i * 128, i * 128 + 128)
        field[base + i, 0:80] = modes[0:80, cols]
        field[base + i, 80:160] = heading[0:80, cols]
        field[base + i, 160:168] = jnp.concatenate([modes[80:84, cols], heading[80:84, cols]], 0)


def greet(space_count, chaos_count, space, chaos):
    barrier = pltpu.get_barrier_semaphore()
    if chaos_count == 4:
        peers = [chaos + 1 - 2 * (chaos % 2), (chaos + 2) % 4]
    else:
        peers = [(chaos + k) % chaos_count for k in range(1, chaos_count)]
    for peer in peers:
        pl.semaphore_signal(
            barrier, inc=1, device_id={"chaos": peer}, device_id_type=pl.DeviceIdType.MESH
        )
    for offset in OFFSETS:
        pl.semaphore_signal(
            barrier, inc=1, device_id={"space": (space + offset + space_count) % space_count},
            device_id_type=pl.DeviceIdType.MESH,
        )
    pl.semaphore_wait(barrier, len(peers) + len(OFFSETS))
    return peers


def spread_modes(chaos_count, peers, chaos, pairs, field, send, recv, meanwhile, early):
    def block(owner, first, count):
        return field.at[pl.ds(owner * pairs + first, count), 0:168]

    if chaos_count == 4:
        across, along = peers
        half = pairs // 2
        plan = [
            (chaos, 0, across), (chaos, half, along),
            (chaos, half, across), (chaos, 0, along),
        ]
        copies = [
            remote(block(o, f, half), block(o, f, half), send.at[i], recv.at[i], {"chaos": t})
            for i, (o, f, t) in enumerate(plan)
        ]
        for copy in copies:
            copy.start()
        meanwhile()
        copies[0].wait_recv()
        on = remote(
            block(across, 0, half), block(across, 0, half), send.at[4], recv.at[4],
            {"chaos": along},
        )
        on.start()
        copies[1].wait_recv()
        over = remote(
            block(along, half, half), block(along, half, half), send.at[5], recv.at[5],
            {"chaos": across},
        )
        over.start()
        early()
        copies[2].wait_recv()
        copies[3].wait_recv()
        on.wait_recv()
        over.wait_recv()
        return copies + [on, over]
    copies = [
        remote(
            block(chaos, 0, pairs), block(chaos, 0, pairs), send.at[i], recv.at[i], {"chaos": t}
        )
        for i, t in enumerate(peers)
    ]
    for copy in copies:
        copy.start()
    meanwhile()
    early()
    for copy in copies:
        copy.wait_recv()
    return copies


def send_halo(space_count, space, picks, field, out, inbox, send, recv):
    low_half = lax.broadcasted_iota(jnp.int32, (1, 128), 1) < 64
    copies = []
    for i, offset in enumerate(OFFSETS):
        target = (space + offset + space_count) % space_count
        e0 = picks[2 * target]
        e1 = picks[2 * target + 1]
        x0 = half_turn(field[e0 // 2], e0 % 2 == 1)
        x1 = half_turn(field[e1 // 2], e1 % 2 == 0)
        out[i] = jnp.where(low_half, x0, x1)
        copy = remote(out.at[i], inbox.at[i], send.at[i], recv.at[i], {"space": target})
        copy.start()
        copies.append(copy)
    return copies


def whole_kernel(
    sizes, picks, k_ref, sensitivity, decay, material, neighbors, modes_far, heading_far,
    nodes_far, weights_far, codes_far, source, res, jvp,
    field, left, right, mass, rhs, kc, acc,
    modes, heading, nodes_t, weights, codes, table, out, inbox,
    send, recv, halo_send, halo_recv, near,
):
    space_count, chaos_count, pairs, halo_depth = sizes
    space = lax.axis_index("space")
    chaos = lax.axis_index("chaos")
    blocks = material.shape[0]
    loads = [
        pltpu.make_async_copy(a, b, near.at[i])
        for i, (a, b) in enumerate(
            [
                (modes_far, modes), (heading_far, heading), (nodes_far, nodes_t),
                (weights_far, weights), (codes_far, codes),
            ]
        )
    ]
    for load in loads:
        load.start()
    fill_aux(k_ref, sensitivity, decay, material, table, field)
    for load in loads:
        load.wait()
    pack_own(modes, heading, pairs, chaos * pairs, field)
    peers = greet(space_count, chaos_count, space, chaos)
    base = chaos * pairs
    ranks = (space, space_count, blocks)

    def early():
        def body(pair, carry):
            pair_first(pair, base, field, left, rhs, kc, acc)
            return carry

        lax.fori_loop(0, pairs, body, 0)

    copies = spread_modes(
        chaos_count, peers, chaos, pairs, field, send, recv,
        lambda: fill_tables(nodes_t, weights, codes, left, right, mass),
        early,
    )
    halo = send_halo(space_count, space, picks, field, out, inbox, halo_send, halo_recv)
    for copy in copies:
        copy.wait_send()
    for i, copy in enumerate(halo):
        copy.wait()
        field[blocks // 2 + i] = inbox[i]

    def late(pair, carry):
        pair_second(
            pair, base, ranks, halo_depth, neighbors, field, left, right, mass, source, res,
            jvp, rhs, kc, acc,
        )
        return carry

    lax.fori_loop(0, pairs, late, 0)


def place_rhs(rhs, face, field, main, tail):
    cols = slice(field * 128, field * 128 + 128)
    row = lax.broadcasted_iota(jnp.int32, (8, 128), 0)
    high = main.astype(BF)
    low = (main - high.astype(F32)).astype(BF)
    tail_high = tail.astype(BF).astype(F32)
    rhs[face, 0:80, cols] = high
    rhs[face, 80:160, cols] = low
    rhs[face, 160:240, cols] = high
    rhs[face, 240:256, cols] = jnp.concatenate(
        [
            jnp.where(row < 4, tail_high, tail - tail_high),
            jnp.where(row < 4, tail_high, 0.0),
        ],
        0,
    ).astype(BF)


def fields(x):
    row = lax.broadcasted_iota(jnp.int32, (8, 128), 0)
    mixed = x[160:168]
    turned = pltpu.roll(mixed, 4, 0)
    mode = (x[0:80], jnp.where(row < 4, mixed, turned))
    step = (x[80:160], jnp.where(row < 4, turned, mixed))
    aux = x[168:176]
    damp = aux[7:8]
    offset = jnp.where(row < 7, aux, 0.0)
    arg_main = mode[0] * damp
    arg_main = jnp.concatenate([arg_main[0:8] + offset, arg_main[8:80]], 0)
    arg = (arg_main, mode[1] * damp)
    rate = damp * LN2
    change = (step[0] * rate, step[1] * rate)
    return mode, step, arg, change


def slot(neighbors, block, face, ranks, halo_depth):
    space, space_count, blocks = ranks
    entry = neighbors[block, face]
    away = jnp.maximum(entry - blocks, 0)
    distance = (space - away // halo_depth + space_count) % space_count
    order = jnp.where(
        distance == 1, 0, jnp.where(distance == space_count - 1, 1, jnp.where(distance == 2, 2, 3))
    )
    index = jnp.where(
        entry >= blocks, blocks + order * halo_depth + away % halo_depth, jnp.maximum(entry, 0)
    )
    return index, jnp.where(entry >= 0, np.float32(0.25), np.float32(0.0))


def face_sum(basis, rhs, face, conduct, change):
    r = jnp.dot(basis, rhs[face], preferred_element_type=F32)
    k = jnp.exp2(r[:, 256:384])
    a = conduct + k
    b = change + k * r[:, 384:512]
    gap = r[:, 0:128]
    return a * gap, b * gap + a * r[:, 128:256]


def place_face(rhs, face, gap, other):
    place_rhs(rhs, face, 0, *gap[0])
    place_rhs(rhs, face, 1, *gap[1])
    place_rhs(rhs, face, 2, *other[2])
    place_rhs(rhs, face, 3, *other[3])


def pair_first(pair, base, field, left, rhs, kc, acc):
    lane = lax.broadcasted_iota(jnp.int32, (1, 128), 1)
    height = lane % 64
    x = field[base + pair]
    mine = fields(x)
    place_rhs(rhs, 6, 0, *mine[2])
    place_rhs(rhs, 6, 1, *mine[3])
    for face in range(2):
        if face == 0:
            scale = jnp.where(height == 63, 0.0, 0.5)
            other = [tuple(pltpu.roll(a, 127, 1) for a in f) for f in mine]
            gap = [tuple((a - b) * scale for a, b in zip(mine[i], other[i])) for i in (0, 1)]
        else:
            scale = jnp.where(height == 0, 1.0, 0.5)
            bottom = height == 0
            other = [tuple(pltpu.roll(a, 1, 1) for a in f) for f in mine]
            gap = [
                tuple((a - jnp.where(bottom, 0.0, b)) * scale for a, b in zip(mine[i], other[i]))
                for i in (0, 1)
            ]
            other = [
                tuple(jnp.where(bottom, a, b) for a, b in zip(mine[i], other[i])) for i in range(4)
            ]
        place_face(rhs, face, gap, other)
    for part in range(left.shape[0] // 512):
        rows = slice(part * 512, part * 512 + 512)
        basis = left[rows]
        r = jnp.dot(basis, rhs[6, :, 0:256], preferred_element_type=F32)
        kc[pair, 0, rows] = jnp.exp2(r[:, 0:128])
        kc[pair, 1, rows] = kc[pair, 0, rows] * r[:, 128:256]
        for face in range(2):
            bal, step = face_sum(basis, rhs, face, kc[pair, 0, rows], kc[pair, 1, rows])
            if face == 0:
                acc[pair, 0, rows] = bal
                acc[pair, 1, rows] = step
            else:
                acc[pair, 0, rows] += bal
                acc[pair, 1, rows] += step


def pair_second(
    pair, base, ranks, halo_depth, neighbors, field, left, right, mass, source, res, jvp, rhs,
    kc, acc,
):
    lane = lax.broadcasted_iota(jnp.int32, (1, 128), 1)
    low_half = lane < 64
    mine = fields(field[base + pair])
    for face in range(2, 6):
        e0, c0 = slot(neighbors, 2 * (base + pair), face - 2, ranks, halo_depth)
        e1, c1 = slot(neighbors, 2 * (base + pair) + 1, face - 2, ranks, halo_depth)
        x0 = half_turn(field[e0 // 2], e0 % 2 == 1)
        x1 = half_turn(field[e1 // 2], e1 % 2 == 0)
        scale = jnp.where(low_half, c0, c1)
        other = fields(jnp.where(low_half, x0, x1))
        gap = [tuple((a - b) * scale for a, b in zip(mine[i], other[i])) for i in (0, 1)]
        place_face(rhs, face, gap, other)
    total = None
    for part in range(left.shape[0] // 512):
        rows = slice(part * 512, part * 512 + 512)
        basis = left[rows]
        for face in range(2, 6):
            bal, step = face_sum(basis, rhs, face, kc[pair, 0, rows], kc[pair, 1, rows])
            acc[pair, 0, rows] += bal
            acc[pair, 1, rows] += step
        both = jnp.concatenate([acc[pair, 0, rows], acc[pair, 1, rows]], 1)
        high = both.astype(BF)
        low = (both - high.astype(F32)).astype(BF)
        w = right[:, rows]
        one = jnp.dot(w, high, preferred_element_type=F32)
        two = jnp.dot(w[0:88], low, preferred_element_type=F32)
        one = one[0:88] + one[88:176] + two
        total = one if total is None else total + one
    cols = pl.ds(pl.multiple_of(pair * 128, 128), 128)
    res[:, cols] = (total[:, 0:128] - mass[...] * source[:, cols])[0:TERMS]
    jvp[:, cols] = total[0:TERMS, 128:256]


def per_device(
    chaos_modes, newton_heading, source, nodes, weights, k_ref, sensitivity, decay,
    material, neighbors, send_list,
):
    space_count = lax.axis_size("space")
    cells = chaos_modes.shape[1]
    pairs = cells // 128
    halo_depth = send_list.shape[2]
    queue = nodes.shape[0]
    blocks = material.shape[0]
    far = pl.BlockSpec(memory_space=pltpu.HBM)
    vmem = pl.BlockSpec(memory_space=pltpu.VMEM)
    smem = pl.BlockSpec(memory_space=pltpu.SMEM)
    return pl.pallas_call(
        functools.partial(
            whole_kernel, (space_count, lax.axis_size("chaos"), pairs, halo_depth)
        ),
        out_shape=[jax.ShapeDtypeStruct((TERMS, cells), F32)] * 2,
        in_specs=[smem] * 6 + [far] * 5 + [vmem],
        out_specs=[vmem] * 2,
        scratch_shapes=[
            pltpu.VMEM((blocks // 2 + 4, 176, 128), F32),
            pltpu.VMEM((queue, 256), BF),
            pltpu.VMEM((176, queue), BF),
            pltpu.VMEM((88, 1), F32),
            pltpu.VMEM((7, 256, 512), BF),
            pltpu.VMEM((pairs, 2, queue, 128), F32),
            pltpu.VMEM((pairs, 2, queue, 128), F32),
            pltpu.VMEM((TERMS, cells), F32),
            pltpu.VMEM((TERMS, cells), F32),
            pltpu.VMEM((nodes.shape[1], queue), F32),
            pltpu.VMEM((1, queue), F32),
            pltpu.VMEM((8, 256), F32),
            pltpu.VMEM((NMAT, 8, 128), F32),
            pltpu.VMEM((4, 176, 128), F32),
            pltpu.VMEM((4, 176, 128), F32),
            pltpu.SemaphoreType.DMA((16,)),
            pltpu.SemaphoreType.DMA((16,)),
            pltpu.SemaphoreType.DMA((4,)),
            pltpu.SemaphoreType.DMA((4,)),
            pltpu.SemaphoreType.DMA((5,)),
        ],
        compiler_params=pltpu.CompilerParams(
            collective_id=0, has_side_effects=True, vmem_limit_bytes=48 * 1024 * 1024
        ),
    )(
        send_list.reshape(-1), k_ref, sensitivity, decay, material, neighbors, chaos_modes,
        newton_heading, nodes.T, weights[None, :], jnp.asarray(order_codes(nodes.shape[1])),
        source[None, :],
    )


def solution(mesh):
    return jax.shard_map(
        per_device,
        mesh=mesh,
        in_specs=(
            P(None, ("space", "chaos")),
            P(None, ("space", "chaos")),
            P(("space", "chaos")),
            P(), P(), P(), P(), P(),
            P("space"),
            P("space", None),
            P("space", None, None),
        ),
        out_specs=(P(None, ("space", "chaos")), P(None, ("space", "chaos"))),
        check_vma=False,
    )
```

```python
import functools
import math

import jax
import jax.numpy as jnp
import numpy as np
from jax import lax
from jax.experimental import pallas as pl
from jax.experimental.pallas import tpu as pltpu
from jax.sharding import PartitionSpec as P

NMAT = 4
SITES = 64
TERMS = 84
MAIN = 80
LOG2E = 1.0 / math.log(2.0)
LN2 = math.log(2.0)
OFFSETS = (1, -1, 2, -2)
BF = jnp.bfloat16
F32 = jnp.float32


def compositions(remaining, places):
    if places == 1:
        return [[remaining]]
    listing = []
    for leading in range(remaining, -1, -1):
        for trailing in compositions(remaining - leading, places - 1):
            listing.append([leading] + trailing)
    return listing


def chaos_orders(variables):
    listing = []
    for degree in range(4):
        listing = listing + compositions(degree, variables)
    return np.array(listing, dtype=np.int32)


def half_turn(x, wanted):
    return jnp.where(wanted, pltpu.roll(x, 64, 1), x)


def factors(x, o):
    second = (x * x - 1.0) * np.float32(1.0 / math.sqrt(2.0))
    third = (x * x * x - 3.0 * x) * np.float32(1.0 / math.sqrt(6.0))
    return jnp.where(o == 0, 1.0, jnp.where(o == 1, x, jnp.where(o == 2, second, third)))


def order_codes(dims):
    orders = chaos_orders(dims)
    code = (orders * 4 ** np.arange(dims)[None, :]).sum(1)
    rest = np.arange(MAIN, TERMS)
    first = np.arange(MAIN)
    column = np.concatenate([first, first, first, rest, rest, rest, np.zeros(4, np.int64)])
    out = np.zeros((8, 256), np.float32)
    out[0] = code[column]
    out[1, :TERMS] = code
    return out


def upright(row):
    return jnp.transpose(jnp.broadcast_to(row, (128, 128)))


def fill_tables(nodes_t, weights, codes, left, right, mass):
    dims = nodes_t.shape[0]
    column = lax.broadcasted_iota(jnp.int32, (1, 128), 1)
    code_right = upright(codes[1:2, 0:128])[0:88].astype(jnp.int32)
    row = lax.broadcasted_iota(jnp.int32, (88, 1), 0)
    mass[...] = jnp.zeros(mass.shape, F32)

    def body(part, carry):
        span = pl.ds(pl.multiple_of(part * 128, 128), 128)
        points = [nodes_t[d : d + 1, span] for d in range(dims)]
        stood = [upright(x) for x in points]
        for side in range(2):
            code = codes[0:1, side * 128 : side * 128 + 128].astype(jnp.int32)
            at = column + side * 128
            lower = ((at >= 160) & (at < 240)) | ((at >= 248) & (at < 252))
            value = None
            for d in range(dims):
                f = factors(stood[d], (code // 4**d) % 4)
                value = f if value is None else value * f
            high = value.astype(BF).astype(F32)
            value = jnp.where(lower, value - high, high)
            left[span, side * 128 : side * 128 + 128] = jnp.where(at < 252, value, 0.0).astype(BF)
        value = weights[:, span]
        for d in range(dims):
            value = value * factors(points[d], (code_right // 4**d) % 4)
        value = jnp.where(row < TERMS, value, 0.0)
        high = value.astype(BF).astype(F32)
        right[:, span] = jnp.concatenate([high, value - high], 0).astype(BF)
        mass[...] += jnp.sum(value, axis=1, keepdims=True)
        return carry

    lax.fori_loop(0, nodes_t.shape[1] // 128, body, 0)


def fill_aux(k_ref, sensitivity, decay, material, table, field):
    row = lax.broadcasted_iota(jnp.int32, (8, 128), 0)
    low_half = lax.broadcasted_iota(jnp.int32, (8, 128), 1) < 64
    dims = sensitivity.shape[1]
    for m in range(NMAT):
        tile = jnp.log(jnp.full((8, 128), k_ref[m], F32))
        for d in range(dims):
            tile = jnp.where(row == d + 1, sensitivity[m, d], tile)
        tile = jnp.where(row == 7, -decay[m], tile)
        table[m] = tile * np.float32(LOG2E)
    for i in range(material.shape[0] // 2):
        field[i, 168:176] = jnp.where(low_half, table[material[2 * i]], table[material[2 * i + 1]])


def remote(src, dst, send, recv, device):
    return pltpu.make_async_remote_copy(
        src_ref=src, dst_ref=dst, send_sem=send, recv_sem=recv,
        device_id=device, device_id_type=pl.DeviceIdType.MESH,
    )


def pack_own(modes, heading, pairs, base, field):
    for i in range(pairs):
        cols = slice(i * 128, i * 128 + 128)
        field[base + i, 0:80] = modes[0:80, cols]
        field[base + i, 80:160] = heading[0:80, cols]
        field[base + i, 160:168] = jnp.concatenate([modes[80:84, cols], heading[80:84, cols]], 0)


def greet(space_count, chaos_count, space, chaos):
    barrier = pltpu.get_barrier_semaphore()
    if chaos_count == 4:
        peers = [chaos + 1 - 2 * (chaos % 2), (chaos + 2) % 4]
    else:
        peers = [(chaos + k) % chaos_count for k in range(1, chaos_count)]
    for peer in peers:
        pl.semaphore_signal(
            barrier, inc=1, device_id={"chaos": peer}, device_id_type=pl.DeviceIdType.MESH
        )
    for offset in OFFSETS:
        pl.semaphore_signal(
            barrier, inc=1, device_id={"space": (space + offset + space_count) % space_count},
            device_id_type=pl.DeviceIdType.MESH,
        )
    pl.semaphore_wait(barrier, len(peers) + len(OFFSETS))
    return peers


def spread_modes(chaos_count, peers, chaos, pairs, field, send, recv, meanwhile, early):
    def block(owner, first, count):
        return field.at[pl.ds(owner * pairs + first, count), 0:168]

    if chaos_count == 4:
        across, along = peers
        half = pairs // 2
        plan = [
            (chaos, 0, across), (chaos, half, along),
            (chaos, half, across), (chaos, 0, along),
        ]
        copies = [
            remote(block(o, f, half), block(o, f, half), send.at[i], recv.at[i], {"chaos": t})
            for i, (o, f, t) in enumerate(plan)
        ]
        for copy in copies:
            copy.start()
        meanwhile()
        copies[0].wait_recv()
        on = remote(
            block(across, 0, half), block(across, 0, half), send.at[4], recv.at[4],
            {"chaos": along},
        )
        on.start()
        copies[1].wait_recv()
        over = remote(
            block(along, half, half), block(along, half, half), send.at[5], recv.at[5],
            {"chaos": across},
        )
        over.start()
        early()
        copies[2].wait_recv()
        copies[3].wait_recv()
        on.wait_recv()
        over.wait_recv()
        return copies + [on, over]
    copies = [
        remote(
            block(chaos, 0, pairs), block(chaos, 0, pairs), send.at[i], recv.at[i], {"chaos": t}
        )
        for i, t in enumerate(peers)
    ]
    for copy in copies:
        copy.start()
    meanwhile()
    early()
    for copy in copies:
        copy.wait_recv()
    return copies


def send_halo(space_count, space, picks, field, out, inbox, send, recv):
    low_half = lax.broadcasted_iota(jnp.int32, (1, 128), 1) < 64
    copies = []
    for i, offset in enumerate(OFFSETS):
        target = (space + offset + space_count) % space_count
        e0 = picks[2 * target]
        e1 = picks[2 * target + 1]
        x0 = half_turn(field[e0 // 2], e0 % 2 == 1)
        x1 = half_turn(field[e1 // 2], e1 % 2 == 0)
        out[i] = jnp.where(low_half, x0, x1)
        copy = remote(out.at[i], inbox.at[i], send.at[i], recv.at[i], {"space": target})
        copy.start()
        copies.append(copy)
    return copies


def whole_kernel(
    sizes, picks, k_ref, sensitivity, decay, material, neighbors, modes_far, heading_far,
    nodes_far, weights_far, codes_far, source, res, jvp,
    field, left, right, mass, rhs, kc, acc,
    modes, heading, nodes_t, weights, codes, table, out, inbox,
    send, recv, halo_send, halo_recv, near,
):
    space_count, chaos_count, pairs, halo_depth = sizes
    space = lax.axis_index("space")
    chaos = lax.axis_index("chaos")
    blocks = material.shape[0]
    loads = [
        pltpu.make_async_copy(a, b, near.at[i])
        for i, (a, b) in enumerate(
            [
                (modes_far, modes), (heading_far, heading), (nodes_far, nodes_t),
                (weights_far, weights), (codes_far, codes),
            ]
        )
    ]
    for load in loads:
        load.start()
    fill_aux(k_ref, sensitivity, decay, material, table, field)
    for load in loads:
        load.wait()
    pack_own(modes, heading, pairs, chaos * pairs, field)
    peers = greet(space_count, chaos_count, space, chaos)
    base = chaos * pairs
    ranks = (space, space_count, blocks)

    def early():
        def body(pair, carry):
            pair_first(pair, base, field, left, rhs, kc, acc)
            return carry

        lax.fori_loop(0, pairs, body, 0)

    copies = spread_modes(
        chaos_count, peers, chaos, pairs, field, send, recv,
        lambda: fill_tables(nodes_t, weights, codes, left, right, mass),
        early,
    )
    halo = send_halo(space_count, space, picks, field, out, inbox, halo_send, halo_recv)
    for copy in copies:
        copy.wait_send()
    for i, copy in enumerate(halo):
        copy.wait()
        field[blocks // 2 + i] = inbox[i]

    def late(pair, carry):
        pair_second(
            pair, base, ranks, halo_depth, neighbors, field, left, right, mass, source, res,
            jvp, rhs, kc, acc,
        )
        return carry

    lax.fori_loop(0, pairs, late, 0)


def place_rhs(rhs, face, field, main, tail):
    cols = slice(field * 128, field * 128 + 128)
    row = lax.broadcasted_iota(jnp.int32, (8, 128), 0)
    high = main.astype(BF)
    low = (main - high.astype(F32)).astype(BF)
    tail_high = tail.astype(BF).astype(F32)
    rhs[face, 0:80, cols] = high
    rhs[face, 80:160, cols] = low
    rhs[face, 160:240, cols] = high
    rhs[face, 240:256, cols] = jnp.concatenate(
        [
            jnp.where(row < 4, tail_high, tail - tail_high),
            jnp.where(row < 4, tail_high, 0.0),
        ],
        0,
    ).astype(BF)


def fields(x):
    row = lax.broadcasted_iota(jnp.int32, (8, 128), 0)
    mixed = x[160:168]
    turned = pltpu.roll(mixed, 4, 0)
    mode = (x[0:80], jnp.where(row < 4, mixed, turned))
    step = (x[80:160], jnp.where(row < 4, turned, mixed))
    aux = x[168:176]
    damp = aux[7:8]
    offset = jnp.where(row < 7, aux, 0.0)
    arg_main = mode[0] * damp
    arg_main = jnp.concatenate([arg_main[0:8] + offset, arg_main[8:80]], 0)
    arg = (arg_main, mode[1] * damp)
    rate = damp * LN2
    change = (step[0] * rate, step[1] * rate)
    return mode, step, arg, change


def slot(neighbors, block, face, ranks, halo_depth):
    space, space_count, blocks = ranks
    entry = neighbors[face, block]
    away = jnp.maximum(entry - blocks, 0)
    distance = (space - away // halo_depth + space_count) % space_count
    order = jnp.where(
        distance == 1, 0, jnp.where(distance == space_count - 1, 1, jnp.where(distance == 2, 2, 3))
    )
    index = jnp.where(
        entry >= blocks, blocks + order * halo_depth + away % halo_depth, jnp.maximum(entry, 0)
    )
    return index, jnp.where(entry >= 0, np.float32(0.25), np.float32(0.0))


def face_sum(basis, rhs, face, conduct, change):
    r = jnp.dot(basis, rhs[face], preferred_element_type=F32)
    k = jnp.exp2(r[:, 256:384])
    a = conduct + k
    b = change + k * r[:, 384:512]
    gap = r[:, 0:128]
    return a * gap, b * gap + a * r[:, 128:256]


def place_face(rhs, face, gap, other):
    place_rhs(rhs, face, 0, *gap[0])
    place_rhs(rhs, face, 1, *gap[1])
    place_rhs(rhs, face, 2, *other[2])
    place_rhs(rhs, face, 3, *other[3])


def pair_first(pair, base, field, left, rhs, kc, acc):
    lane = lax.broadcasted_iota(jnp.int32, (1, 128), 1)
    height = lane % 64
    x = field[base + pair]
    mine = fields(x)
    place_rhs(rhs, 6, 0, *mine[2])
    place_rhs(rhs, 6, 1, *mine[3])
    for face in range(2):
        if face == 0:
            scale = jnp.where(height == 63, 0.0, 0.5)
            other = [tuple(pltpu.roll(a, 127, 1) for a in f) for f in mine]
            gap = [tuple((a - b) * scale for a, b in zip(mine[i], other[i])) for i in (0, 1)]
        else:
            scale = jnp.where(height == 0, 1.0, 0.5)
            bottom = height == 0
            other = [tuple(pltpu.roll(a, 1, 1) for a in f) for f in mine]
            gap = [
                tuple((a - jnp.where(bottom, 0.0, b)) * scale for a, b in zip(mine[i], other[i]))
                for i in (0, 1)
            ]
            other = [
                tuple(jnp.where(bottom, a, b) for a, b in zip(mine[i], other[i])) for i in range(4)
            ]
        place_face(rhs, face, gap, other)
    for part in range(left.shape[0] // 512):
        rows = slice(part * 512, part * 512 + 512)
        basis = left[rows]
        r = jnp.dot(basis, rhs[6, :, 0:256], preferred_element_type=F32)
        kc[pair, 0, rows] = jnp.exp2(r[:, 0:128])
        kc[pair, 1, rows] = kc[pair, 0, rows] * r[:, 128:256]
        for face in range(2):
            bal, step = face_sum(basis, rhs, face, kc[pair, 0, rows], kc[pair, 1, rows])
            if face == 0:
                acc[pair, 0, rows] = bal
                acc[pair, 1, rows] = step
            else:
                acc[pair, 0, rows] += bal
                acc[pair, 1, rows] += step


def pair_second(
    pair, base, ranks, halo_depth, neighbors, field, left, right, mass, source, res, jvp, rhs,
    kc, acc,
):
    lane = lax.broadcasted_iota(jnp.int32, (1, 128), 1)
    low_half = lane < 64
    mine = fields(field[base + pair])
    for face in range(2, 6):
        e0, c0 = slot(neighbors, 2 * (base + pair), face - 2, ranks, halo_depth)
        e1, c1 = slot(neighbors, 2 * (base + pair) + 1, face - 2, ranks, halo_depth)
        x0 = half_turn(field[e0 // 2], e0 % 2 == 1)
        x1 = half_turn(field[e1 // 2], e1 % 2 == 0)
        scale = jnp.where(low_half, c0, c1)
        other = fields(jnp.where(low_half, x0, x1))
        gap = [tuple((a - b) * scale for a, b in zip(mine[i], other[i])) for i in (0, 1)]
        place_face(rhs, face, gap, other)
    total = None
    for part in range(left.shape[0] // 512):
        rows = slice(part * 512, part * 512 + 512)
        basis = left[rows]
        for face in range(2, 6):
            bal, step = face_sum(basis, rhs, face, kc[pair, 0, rows], kc[pair, 1, rows])
            acc[pair, 0, rows] += bal
            acc[pair, 1, rows] += step
        both = jnp.concatenate([acc[pair, 0, rows], acc[pair, 1, rows]], 1)
        high = both.astype(BF)
        low = (both - high.astype(F32)).astype(BF)
        w = right[:, rows]
        one = jnp.dot(w, high, preferred_element_type=F32)
        two = jnp.dot(w[0:88], low, preferred_element_type=F32)
        one = one[0:88] + one[88:176] + two
        total = one if total is None else total + one
    cols = pl.ds(pl.multiple_of(pair * 128, 128), 128)
    res[:, cols] = (total[:, 0:128] - mass[...] * source[:, cols])[0:TERMS]
    jvp[:, cols] = total[0:TERMS, 128:256]


def per_device(
    chaos_modes, newton_heading, source, nodes, weights, k_ref, sensitivity, decay,
    material, neighbors, send_list,
):
    space_count = lax.axis_size("space")
    cells = chaos_modes.shape[1]
    pairs = cells // 128
    halo_depth = send_list.shape[2]
    queue = nodes.shape[0]
    blocks = material.shape[0]
    far = pl.BlockSpec(memory_space=pltpu.HBM)
    vmem = pl.BlockSpec(memory_space=pltpu.VMEM)
    smem = pl.BlockSpec(memory_space=pltpu.SMEM)
    return pl.pallas_call(
        functools.partial(
            whole_kernel, (space_count, lax.axis_size("chaos"), pairs, halo_depth)
        ),
        out_shape=[jax.ShapeDtypeStruct((TERMS, cells), F32)] * 2,
        in_specs=[smem] * 6 + [far] * 5 + [vmem],
        out_specs=[vmem] * 2,
        scratch_shapes=[
            pltpu.VMEM((blocks // 2 + 4, 176, 128), F32),
            pltpu.VMEM((queue, 256), BF),
            pltpu.VMEM((176, queue), BF),
            pltpu.VMEM((88, 1), F32),
            pltpu.VMEM((7, 256, 512), BF),
            pltpu.VMEM((pairs, 2, queue, 128), F32),
            pltpu.VMEM((pairs, 2, queue, 128), F32),
            pltpu.VMEM((TERMS, cells), F32),
            pltpu.VMEM((TERMS, cells), F32),
            pltpu.VMEM((nodes.shape[1], queue), F32),
            pltpu.VMEM((1, queue), F32),
            pltpu.VMEM((8, 256), F32),
            pltpu.VMEM((NMAT, 8, 128), F32),
            pltpu.VMEM((4, 176, 128), F32),
            pltpu.VMEM((4, 176, 128), F32),
            pltpu.SemaphoreType.DMA((16,)),
            pltpu.SemaphoreType.DMA((16,)),
            pltpu.SemaphoreType.DMA((4,)),
            pltpu.SemaphoreType.DMA((4,)),
            pltpu.SemaphoreType.DMA((5,)),
        ],
        compiler_params=pltpu.CompilerParams(
            collective_id=0, has_side_effects=True, vmem_limit_bytes=60 * 1024 * 1024
        ),
    )(
        send_list.reshape(-1), k_ref, sensitivity, decay, material, neighbors.T, chaos_modes,
        newton_heading, nodes.T, weights[None, :], jnp.asarray(order_codes(nodes.shape[1])),
        source[None, :],
    )


def solution(mesh):
    return jax.shard_map(
        per_device,
        mesh=mesh,
        in_specs=(
            P(None, ("space", "chaos")),
            P(None, ("space", "chaos")),
            P(("space", "chaos")),
            P(), P(), P(), P(), P(),
            P("space"),
            P("space", None),
            P("space", None, None),
        ),
        out_specs=(P(None, ("space", "chaos")), P(None, ("space", "chaos"))),
        check_vma=False,
    )
```

```python
import functools
import math

import jax
import jax.numpy as jnp
import numpy as np
from jax import lax
from jax.experimental import pallas as pl
from jax.experimental.pallas import tpu as pltpu
from jax.sharding import PartitionSpec as P

NMAT = 4
SITES = 64
TERMS = 84
MAIN = 80
LOG2E = 1.0 / math.log(2.0)
LN2 = math.log(2.0)
OFFSETS = (1, -1, 2, -2)
BF = jnp.bfloat16
F32 = jnp.float32


def compositions(remaining, places):
    if places == 1:
        return [[remaining]]
    listing = []
    for leading in range(remaining, -1, -1):
        for trailing in compositions(remaining - leading, places - 1):
            listing.append([leading] + trailing)
    return listing


def chaos_orders(variables):
    listing = []
    for degree in range(4):
        listing = listing + compositions(degree, variables)
    return np.array(listing, dtype=np.int32)


def half_turn(x, wanted):
    return jnp.where(wanted, pltpu.roll(x, 64, 1), x)


def factors(x, o):
    second = (x * x - 1.0) * np.float32(1.0 / math.sqrt(2.0))
    third = (x * x * x - 3.0 * x) * np.float32(1.0 / math.sqrt(6.0))
    return jnp.where(o == 0, 1.0, jnp.where(o == 1, x, jnp.where(o == 2, second, third)))


def order_codes(dims):
    orders = chaos_orders(dims)
    code = (orders * 4 ** np.arange(dims)[None, :]).sum(1)
    rest = np.arange(MAIN, TERMS)
    first = np.arange(MAIN)
    column = np.concatenate([first, first, first, rest, rest, rest, np.zeros(4, np.int64)])
    out = np.zeros((8, 256), np.float32)
    out[0] = code[column]
    out[1, :TERMS] = code
    return out


def upright(row):
    return jnp.transpose(jnp.broadcast_to(row, (128, 128)))


def fill_tables(nodes_t, weights, codes, left, right, mass):
    dims = nodes_t.shape[0]
    column = lax.broadcasted_iota(jnp.int32, (1, 128), 1)
    code_right = upright(codes[1:2, 0:128])[0:88].astype(jnp.int32)
    row = lax.broadcasted_iota(jnp.int32, (88, 1), 0)
    mass[...] = jnp.zeros(mass.shape, F32)

    def body(part, carry):
        span = pl.ds(pl.multiple_of(part * 128, 128), 128)
        points = [nodes_t[d : d + 1, span] for d in range(dims)]
        stood = [upright(x) for x in points]
        for side in range(2):
            code = codes[0:1, side * 128 : side * 128 + 128].astype(jnp.int32)
            at = column + side * 128
            lower = ((at >= 160) & (at < 240)) | ((at >= 248) & (at < 252))
            value = None
            for d in range(dims):
                f = factors(stood[d], (code // 4**d) % 4)
                value = f if value is None else value * f
            high = value.astype(BF).astype(F32)
            value = jnp.where(lower, value - high, high)
            left[span, side * 128 : side * 128 + 128] = jnp.where(at < 252, value, 0.0).astype(BF)
        value = weights[:, span]
        for d in range(dims):
            value = value * factors(points[d], (code_right // 4**d) % 4)
        value = jnp.where(row < TERMS, value, 0.0)
        high = value.astype(BF).astype(F32)
        right[:, span] = jnp.concatenate([high, value - high], 0).astype(BF)
        mass[...] += jnp.sum(value, axis=1, keepdims=True)
        return carry

    lax.fori_loop(0, nodes_t.shape[1] // 128, body, 0)


def fill_aux(k_ref, sensitivity, decay, material, table, field):
    row = lax.broadcasted_iota(jnp.int32, (8, 128), 0)
    low_half = lax.broadcasted_iota(jnp.int32, (8, 128), 1) < 64
    dims = sensitivity.shape[1]
    for m in range(NMAT):
        tile = jnp.log(jnp.full((8, 128), k_ref[m], F32))
        for d in range(dims):
            tile = jnp.where(row == d + 1, sensitivity[m, d], tile)
        tile = jnp.where(row == 7, -decay[m], tile)
        table[m] = tile * np.float32(LOG2E)
    for i in range(material.shape[0] // 2):
        field[i, 168:176] = jnp.where(low_half, table[material[2 * i]], table[material[2 * i + 1]])


def remote(src, dst, send, recv, device):
    return pltpu.make_async_remote_copy(
        src_ref=src, dst_ref=dst, send_sem=send, recv_sem=recv,
        device_id=device, device_id_type=pl.DeviceIdType.MESH,
    )


def pack_own(modes, heading, pairs, base, field):
    for i in range(pairs):
        cols = slice(i * 128, i * 128 + 128)
        field[base + i, 0:80] = modes[0:80, cols]
        field[base + i, 80:160] = heading[0:80, cols]
        field[base + i, 160:168] = jnp.concatenate([modes[80:84, cols], heading[80:84, cols]], 0)


def greet(space_count, chaos_count, space, chaos):
    barrier = pltpu.get_barrier_semaphore()
    if chaos_count == 4:
        peers = [chaos + 1 - 2 * (chaos % 2), (chaos + 2) % 4]
    else:
        peers = [(chaos + k) % chaos_count for k in range(1, chaos_count)]
    for peer in peers:
        pl.semaphore_signal(
            barrier, inc=1, device_id={"chaos": peer}, device_id_type=pl.DeviceIdType.MESH
        )
    for offset in OFFSETS:
        pl.semaphore_signal(
            barrier, inc=1, device_id={"space": (space + offset + space_count) % space_count},
            device_id_type=pl.DeviceIdType.MESH,
        )
    return barrier, peers


def spread_modes(chaos_count, peers, chaos, pairs, field, send, recv, meanwhile, early):
    def block(owner, first, count):
        return field.at[pl.ds(owner * pairs + first, count), 0:168]

    if chaos_count == 4:
        across, along = peers
        half = pairs // 2
        plan = [
            (chaos, 0, across), (chaos, half, along),
            (chaos, half, across), (chaos, 0, along),
        ]
        copies = [
            remote(block(o, f, half), block(o, f, half), send.at[i], recv.at[i], {"chaos": t})
            for i, (o, f, t) in enumerate(plan)
        ]
        for copy in copies:
            copy.start()
        meanwhile()
        copies[0].wait_recv()
        on = remote(
            block(across, 0, half), block(across, 0, half), send.at[4], recv.at[4],
            {"chaos": along},
        )
        on.start()
        copies[1].wait_recv()
        over = remote(
            block(along, half, half), block(along, half, half), send.at[5], recv.at[5],
            {"chaos": across},
        )
        over.start()
        early()
        copies[2].wait_recv()
        copies[3].wait_recv()
        on.wait_recv()
        over.wait_recv()
        return copies + [on, over]
    copies = [
        remote(
            block(chaos, 0, pairs), block(chaos, 0, pairs), send.at[i], recv.at[i], {"chaos": t}
        )
        for i, t in enumerate(peers)
    ]
    for copy in copies:
        copy.start()
    meanwhile()
    early()
    for copy in copies:
        copy.wait_recv()
    return copies


def send_halo(space_count, space, picks, field, out, inbox, send, recv):
    low_half = lax.broadcasted_iota(jnp.int32, (1, 128), 1) < 64
    copies = []
    for i, offset in enumerate(OFFSETS):
        target = (space + offset + space_count) % space_count
        e0 = picks[2 * target]
        e1 = picks[2 * target + 1]
        x0 = half_turn(field[e0 // 2], e0 % 2 == 1)
        x1 = half_turn(field[e1 // 2], e1 % 2 == 0)
        out[i] = jnp.where(low_half, x0, x1)
        copy = remote(out.at[i], inbox.at[i], send.at[i], recv.at[i], {"space": target})
        copy.start()
        copies.append(copy)
    return copies


def whole_kernel(
    sizes, picks, k_ref, sensitivity, decay, material, neighbors, modes_far, heading_far,
    nodes_far, weights_far, codes_far, source, res, jvp,
    field, left, right, mass, rhs, kc, acc,
    modes, heading, nodes_t, weights, codes, table, out, inbox,
    send, recv, halo_send, halo_recv, near,
):
    space_count, chaos_count, pairs, halo_depth = sizes
    space = lax.axis_index("space")
    chaos = lax.axis_index("chaos")
    blocks = material.shape[0]
    barrier, peers = greet(space_count, chaos_count, space, chaos)
    loads = [
        pltpu.make_async_copy(a, b, near.at[i])
        for i, (a, b) in enumerate(
            [
                (modes_far, modes), (heading_far, heading), (nodes_far, nodes_t),
                (weights_far, weights), (codes_far, codes),
            ]
        )
    ]
    for load in loads:
        load.start()
    fill_aux(k_ref, sensitivity, decay, material, table, field)
    for load in loads:
        load.wait()
    pack_own(modes, heading, pairs, chaos * pairs, field)
    pl.semaphore_wait(barrier, len(peers) + len(OFFSETS))
    base = chaos * pairs
    ranks = (space, space_count, blocks)

    def early():
        def body(pair, carry):
            pair_first(pair, base, field, left, rhs, kc, acc)
            return carry

        lax.fori_loop(0, pairs, body, 0)

    copies = spread_modes(
        chaos_count, peers, chaos, pairs, field, send, recv,
        lambda: fill_tables(nodes_t, weights, codes, left, right, mass),
        early,
    )
    halo = send_halo(space_count, space, picks, field, out, inbox, halo_send, halo_recv)
    for copy in copies:
        copy.wait_send()
    for i, copy in enumerate(halo):
        copy.wait()
        field[blocks // 2 + i] = inbox[i]

    def late(pair, carry):
        pair_second(
            pair, base, ranks, halo_depth, neighbors, field, left, right, mass, source, res,
            jvp, rhs, kc, acc,
        )
        return carry

    lax.fori_loop(0, pairs, late, 0)


def place_rhs(rhs, face, field, main, tail):
    cols = slice(field * 128, field * 128 + 128)
    row = lax.broadcasted_iota(jnp.int32, (8, 128), 0)
    high = main.astype(BF)
    low = (main - high.astype(F32)).astype(BF)
    tail_high = tail.astype(BF).astype(F32)
    rhs[face, 0:80, cols] = high
    rhs[face, 80:160, cols] = low
    rhs[face, 160:240, cols] = high
    rhs[face, 240:256, cols] = jnp.concatenate(
        [
            jnp.where(row < 4, tail_high, tail - tail_high),
            jnp.where(row < 4, tail_high, 0.0),
        ],
        0,
    ).astype(BF)


def fields(x):
    row = lax.broadcasted_iota(jnp.int32, (8, 128), 0)
    mixed = x[160:168]
    turned = pltpu.roll(mixed, 4, 0)
    mode = (x[0:80], jnp.where(row < 4, mixed, turned))
    step = (x[80:160], jnp.where(row < 4, turned, mixed))
    aux = x[168:176]
    damp = aux[7:8]
    offset = jnp.where(row < 7, aux, 0.0)
    arg_main = mode[0] * damp
    arg_main = jnp.concatenate([arg_main[0:8] + offset, arg_main[8:80]], 0)
    arg = (arg_main, mode[1] * damp)
    rate = damp * LN2
    change = (step[0] * rate, step[1] * rate)
    return mode, step, arg, change


def slot(neighbors, block, face, ranks, halo_depth):
    space, space_count, blocks = ranks
    entry = neighbors[face, block]
    away = jnp.maximum(entry - blocks, 0)
    distance = (space - away // halo_depth + space_count) % space_count
    order = jnp.where(
        distance == 1, 0, jnp.where(distance == space_count - 1, 1, jnp.where(distance == 2, 2, 3))
    )
    index = jnp.where(
        entry >= blocks, blocks + order * halo_depth + away % halo_depth, jnp.maximum(entry, 0)
    )
    return index, jnp.where(entry >= 0, np.float32(0.25), np.float32(0.0))


def face_sum(basis, rhs, face, conduct, change):
    r = jnp.dot(basis, rhs[face], preferred_element_type=F32)
    k = jnp.exp2(r[:, 256:384])
    a = conduct + k
    b = change + k * r[:, 384:512]
    gap = r[:, 0:128]
    return a * gap, b * gap + a * r[:, 128:256]


def place_face(rhs, face, gap, other):
    place_rhs(rhs, face, 0, *gap[0])
    place_rhs(rhs, face, 1, *gap[1])
    place_rhs(rhs, face, 2, *other[2])
    place_rhs(rhs, face, 3, *other[3])


def pair_first(pair, base, field, left, rhs, kc, acc):
    lane = lax.broadcasted_iota(jnp.int32, (1, 128), 1)
    height = lane % 64
    x = field[base + pair]
    mine = fields(x)
    place_rhs(rhs, 6, 0, *mine[2])
    place_rhs(rhs, 6, 1, *mine[3])
    for face in range(2):
        if face == 0:
            scale = jnp.where(height == 63, 0.0, 0.5)
            other = [tuple(pltpu.roll(a, 127, 1) for a in f) for f in mine]
            gap = [tuple((a - b) * scale for a, b in zip(mine[i], other[i])) for i in (0, 1)]
        else:
            scale = jnp.where(height == 0, 1.0, 0.5)
            bottom = height == 0
            other = [tuple(pltpu.roll(a, 1, 1) for a in f) for f in mine]
            gap = [
                tuple((a - jnp.where(bottom, 0.0, b)) * scale for a, b in zip(mine[i], other[i]))
                for i in (0, 1)
            ]
            other = [
                tuple(jnp.where(bottom, a, b) for a, b in zip(mine[i], other[i])) for i in range(4)
            ]
        place_face(rhs, face, gap, other)
    for part in range(left.shape[0] // 512):
        rows = slice(part * 512, part * 512 + 512)
        basis = left[rows]
        r = jnp.dot(basis, rhs[6, :, 0:256], preferred_element_type=F32)
        kc[pair, 0, rows] = jnp.exp2(r[:, 0:128])
        kc[pair, 1, rows] = kc[pair, 0, rows] * r[:, 128:256]
        for face in range(2):
            bal, step = face_sum(basis, rhs, face, kc[pair, 0, rows], kc[pair, 1, rows])
            if face == 0:
                acc[pair, 0, rows] = bal
                acc[pair, 1, rows] = step
            else:
                acc[pair, 0, rows] += bal
                acc[pair, 1, rows] += step


def pair_second(
    pair, base, ranks, halo_depth, neighbors, field, left, right, mass, source, res, jvp, rhs,
    kc, acc,
):
    lane = lax.broadcasted_iota(jnp.int32, (1, 128), 1)
    low_half = lane < 64
    mine = fields(field[base + pair])
    for face in range(2, 6):
        e0, c0 = slot(neighbors, 2 * (base + pair), face - 2, ranks, halo_depth)
        e1, c1 = slot(neighbors, 2 * (base + pair) + 1, face - 2, ranks, halo_depth)
        x0 = half_turn(field[e0 // 2], e0 % 2 == 1)
        x1 = half_turn(field[e1 // 2], e1 % 2 == 0)
        scale = jnp.where(low_half, c0, c1)
        other = fields(jnp.where(low_half, x0, x1))
        gap = [tuple((a - b) * scale for a, b in zip(mine[i], other[i])) for i in (0, 1)]
        place_face(rhs, face, gap, other)
    total = None
    for part in range(left.shape[0] // 512):
        rows = slice(part * 512, part * 512 + 512)
        basis = left[rows]
        for face in range(2, 6):
            bal, step = face_sum(basis, rhs, face, kc[pair, 0, rows], kc[pair, 1, rows])
            acc[pair, 0, rows] += bal
            acc[pair, 1, rows] += step
        both = jnp.concatenate([acc[pair, 0, rows], acc[pair, 1, rows]], 1)
        high = both.astype(BF)
        low = (both - high.astype(F32)).astype(BF)
        w = right[:, rows]
        one = jnp.dot(w, high, preferred_element_type=F32)
        two = jnp.dot(w[0:88], low, preferred_element_type=F32)
        one = one[0:88] + one[88:176] + two
        total = one if total is None else total + one
    cols = pl.ds(pl.multiple_of(pair * 128, 128), 128)
    res[:, cols] = (total[:, 0:128] - mass[...] * source[:, cols])[0:TERMS]
    jvp[:, cols] = total[0:TERMS, 128:256]


def per_device(
    chaos_modes, newton_heading, source, nodes, weights, k_ref, sensitivity, decay,
    material, neighbors, send_list,
):
    space_count = lax.axis_size("space")
    cells = chaos_modes.shape[1]
    pairs = cells // 128
    halo_depth = send_list.shape[2]
    queue = nodes.shape[0]
    blocks = material.shape[0]
    far = pl.BlockSpec(memory_space=pltpu.HBM)
    vmem = pl.BlockSpec(memory_space=pltpu.VMEM)
    smem = pl.BlockSpec(memory_space=pltpu.SMEM)
    return pl.pallas_call(
        functools.partial(
            whole_kernel, (space_count, lax.axis_size("chaos"), pairs, halo_depth)
        ),
        out_shape=[jax.ShapeDtypeStruct((TERMS, cells), F32)] * 2,
        in_specs=[smem] * 6 + [far] * 5 + [vmem],
        out_specs=[vmem] * 2,
        scratch_shapes=[
            pltpu.VMEM((blocks // 2 + 4, 176, 128), F32),
            pltpu.VMEM((queue, 256), BF),
            pltpu.VMEM((176, queue), BF),
            pltpu.VMEM((88, 1), F32),
            pltpu.VMEM((7, 256, 512), BF),
            pltpu.VMEM((pairs, 2, queue, 128), F32),
            pltpu.VMEM((pairs, 2, queue, 128), F32),
            pltpu.VMEM((TERMS, cells), F32),
            pltpu.VMEM((TERMS, cells), F32),
            pltpu.VMEM((nodes.shape[1], queue), F32),
            pltpu.VMEM((1, queue), F32),
            pltpu.VMEM((8, 256), F32),
            pltpu.VMEM((NMAT, 8, 128), F32),
            pltpu.VMEM((4, 176, 128), F32),
            pltpu.VMEM((4, 176, 128), F32),
            pltpu.SemaphoreType.DMA((16,)),
            pltpu.SemaphoreType.DMA((16,)),
            pltpu.SemaphoreType.DMA((4,)),
            pltpu.SemaphoreType.DMA((4,)),
            pltpu.SemaphoreType.DMA((5,)),
        ],
        compiler_params=pltpu.CompilerParams(
            collective_id=0, has_side_effects=True, vmem_limit_bytes=60 * 1024 * 1024
        ),
    )(
        send_list.reshape(-1), k_ref, sensitivity, decay, material, neighbors.T, chaos_modes,
        newton_heading, nodes.T, weights[None, :], jnp.asarray(order_codes(nodes.shape[1])),
        source[None, :],
    )


def solution(mesh):
    return jax.shard_map(
        per_device,
        mesh=mesh,
        in_specs=(
            P(None, ("space", "chaos")),
            P(None, ("space", "chaos")),
            P(("space", "chaos")),
            P(), P(), P(), P(), P(),
            P("space"),
            P("space", None),
            P("space", None, None),
        ),
        out_specs=(P(None, ("space", "chaos")), P(None, ("space", "chaos"))),
        check_vma=False,
    )
```
